32 devices in a mesh: col: 4 (over z), row: 8 (over y, x, core).
Axes of the slice: x: 2, y: 2, z: 4, core: 2. Of those that a mesh axis runs over, the one named last changes fastest.
Arguments:
- factor: float32 [8192, 2048], P('row', 'col'), may hold values from -100 to 100
- support: int32 [16, 64], P(None, 'row'), may hold values from 0 to 1, as said below
- plan: int32 [2, 16], replicated, may hold values from 0 to 15, as said below
Outputs:
- rotated_factor: float32 [8192, 2048], P('row', 'col')
The draws below stay inside these ranges and needn't reach their ends.
Inputs may be any that keep to these rules, and one draw needn't show every extreme that they name: Every column block has at least one row block in its support. `plan`: each row is a permutation; cut each round's row into groups of 4 consecutive positions (group g on index g of col); the 4 blocks of any group sit in 4 different groups of the previous round's row, where the order before round 0 is 0, 1, ..., 15.
All inputs are finite; a program needn't handle non-finite values.
Results may differ from the reference program's by a relative error of at most 0.0003.
Values sent between devices are 32-bit elements; how exact they have to be, the bound alone decides.
A program may use at most 128 MiB of HBM per device.

```python
import math
import jax
import jax.numpy as jnp
from jax import lax

W = 128
NCB = 16
RB = 128
ROUNDS = 2
NB = 64
ROWS = 8192
COLS = 2048
N_COL = 4


def draw_factor(key, part):
    keys = jax.random.split(key, 5)
    row_scale = jnp.exp(jax.random.uniform(keys[0], (ROWS, 1), jnp.float32, math.log(0.3), math.log(3.0)))
    col_scale = jnp.exp(jax.random.uniform(keys[1], (1, COLS), jnp.float32, math.log(0.3), math.log(3.0)))
    loading = jax.random.uniform(keys[2], (1, COLS), jnp.float32, -1.5, 1.5)
    common = jnp.clip(jax.random.normal(keys[3], (ROWS, 1), jnp.float32), -4.0, 4.0)
    noise = jnp.clip(jax.random.normal(keys[4], (ROWS, COLS), jnp.float32), -4.0, 4.0)
    return (row_scale * col_scale * (common * loading + noise)).astype(jnp.float32)


def draw_support(key, part):
    vote_key, anchor_key = jax.random.split(key)
    block_ids = jnp.arange(NB, dtype=jnp.int32)
    threshold = 25 + 70 * block_ids // NB
    votes = jax.random.randint(vote_key, (NCB, NB), 0, 100)
    anchors = jax.random.randint(anchor_key, (NCB, 1), 0, NB)
    chosen = jnp.logical_or(votes < threshold[None, :], block_ids[None, :] == anchors)
    return jnp.where(chosen, 1, 0).astype(jnp.int32)


def draw_plan(key, part):
    group_count = N_COL
    previous = jnp.arange(NCB, dtype=jnp.int32)
    rounds_list = []

    def shuffled(one_key):
        return jax.random.permutation(one_key, group_count)
    for round_index in range(ROUNDS):
        round_key = jax.random.fold_in(key, round_index)
        shift_key, order_key = jax.random.split(round_key)
        offsets = jax.random.permutation(shift_key, group_count)
        inner = jax.vmap(shuffled)(jax.random.split(order_key, group_count))
        targets = jnp.broadcast_to(jnp.arange(group_count)[:, None], (group_count, group_count))
        slot_ids = jnp.broadcast_to(jnp.arange(group_count)[None, :], (group_count, group_count))
        sources = (targets + offsets[slot_ids]) % group_count
        local_ids = inner[sources, targets]
        previous = previous[(sources * group_count + local_ids).reshape(NCB)]
        rounds_list.append(previous)
    return jnp.stack(rounds_list).astype(jnp.int32)


def setup_inputs(seed: int = 0) -> dict:
    seeds = jax.random.split(jax.random.key(seed), 4)
    factor = draw_factor(jax.random.fold_in(seeds[3], 71), 0)
    support = draw_support(jax.random.fold_in(seeds[3], 71), 0)
    plan = draw_plan(jax.random.fold_in(seeds[3], 71), 0)
    return dict(factor=factor, support=support, plan=plan)


precise = lax.Precision.HIGHEST
damping = 0.01

def skew_terms(gram_rows, diag_rows, diag_cols):
    spread = diag_rows[:, :, None] - diag_cols[:, None, :]
    joined = diag_rows[:, :, None] + diag_cols[:, None, :]
    return gram_rows * spread / (spread * spread + gram_rows * gram_rows + damping * joined * joined)

def cayley(skew_matrix):
    size_here = skew_matrix.shape[0]
    identity = jnp.eye(size_here, dtype=jnp.float32)
    halved = 0.5 * skew_matrix
    minus_half = identity - halved
    numerator = jnp.dot(minus_half, minus_half, precision=precise)
    definite = identity + jnp.dot(halved.T, halved, precision=precise)
    lower_factor = jnp.linalg.cholesky(definite)
    return jax.scipy.linalg.cho_solve((lower_factor, True), numerator)

def reference(factor, support, plan):
    total_rows = factor.shape[0]
    row_mask = jnp.repeat(support.T, RB, axis=0).astype(jnp.float32)
    current = factor.reshape(total_rows, NCB, W) * row_mask[:, :, None]
    previous = jnp.arange(NCB, dtype=jnp.int32)
    for round_index in range(ROUNDS):
        order_now = plan[round_index]
        located = jnp.argsort(previous)[order_now]
        arranged = current[:, located, :]
        paired = arranged.reshape(total_rows, NCB // 2, 2 * W)
        gram_matrix = jnp.einsum('rpi,rpj->pij', paired, paired, precision=precise)
        diagonal_terms = jnp.diagonal(gram_matrix, axis1=1, axis2=2)
        skew_matrix = skew_terms(gram_matrix, diagonal_terms, diagonal_terms)
        rotations = jax.vmap(cayley)(skew_matrix)
        rotated = jnp.einsum('rpi,pij->rpj', paired, rotations, precision=precise)
        current = rotated.reshape(total_rows, NCB, W)
        previous = order_now
    return current.reshape(total_rows, NCB * W)
```

```python
import functools

import jax
import jax.numpy as jnp
from jax import lax
from jax.experimental import pallas as pl
from jax.experimental.pallas import tpu as pltpu
from jax.sharding import PartitionSpec as P

W = 128
RB = 128
ROUNDS = 2
CHUNKS = 4
SCALED_STEPS = 7
TRUE_STEPS = 2
DAMPING = 0.01
F32 = jnp.float32
BF16 = jnp.bfloat16
MESH = pl.DeviceIdType.MESH


def split(x):
    high = x.astype(BF16)
    return high, (x - high.astype(F32)).astype(BF16)


def dot(a, b):
    return jnp.dot(a, b, preferred_element_type=F32)


def dot3(a, b):
    a_high, a_low = split(a)
    b_high, b_low = split(b)
    return dot(a_high, b_high) + (dot(a_high, b_low) + dot(a_low, b_high))


def dot_t(a, b):
    return lax.dot_general(a, b, (((0,), (0,)), ((), ())), preferred_element_type=F32)


def rotation(gram, eye, stack):
    size = gram.shape[0]
    on_diagonal = gram * eye
    diag_rows = jnp.sum(on_diagonal, axis=1, keepdims=True)
    diag_cols = jnp.sum(on_diagonal, axis=0, keepdims=True)
    spread = diag_rows - diag_cols
    joined = diag_rows + diag_cols
    half = 0.5 * gram * spread / (spread * spread + gram * gram + DAMPING * joined * joined)
    squared = dot3(half, half)
    total = jnp.sum(jnp.sum(squared * squared, axis=1, keepdims=True), axis=0, keepdims=True)
    upper = 1.0 + 1.001 * jnp.sqrt(0.5 * total)
    stack[:size] = eye - squared
    stack[size:] = eye - half

    def scaled(_, bounds):
        low, high = bounds
        scale = 2.0 / (low + high)
        delta = (high - low) / (high + low)
        factor = (2.0 * scale) * eye - (scale * scale) * stack[:size]
        stack[...] = dot3(stack[...], factor)
        return 1.0 - delta * delta, jnp.ones_like(high)

    lax.fori_loop(0, SCALED_STEPS, scaled, (jnp.ones_like(upper), upper))

    def true(_, carry):
        inverse = stack[size:]
        residual = (eye - inverse) - dot3(half, inverse)
        stack[size:] = inverse + dot3(inverse, residual)
        return carry

    lax.fori_loop(0, TRUE_STEPS, true, 0)
    return 2.0 * stack[size:] - eye


def pack(gram):
    first, last = gram[:W, :W], gram[W:, W:]
    row_ids = lax.broadcasted_iota(jnp.int32, (W, W), 0)
    col_ids = lax.broadcasted_iota(jnp.int32, (W, W), 1)
    tile = jnp.where(row_ids >= col_ids, first, last)
    diagonal = jnp.sum(jnp.where(row_ids == col_ids, last, 0.0), axis=0, keepdims=True)
    return gram[:W, W:], tile, jnp.broadcast_to(diagonal, (8, W))


def unpack(packed):
    cross, tile, diagonal = packed[:W], packed[W:2 * W], packed[2 * W:2 * W + 1]
    row_ids = lax.broadcasted_iota(jnp.int32, (W, W), 0)
    col_ids = lax.broadcasted_iota(jnp.int32, (W, W), 1)
    lower = jnp.where(row_ids > col_ids, tile, 0.0)
    upper = jnp.where(row_ids < col_ids, tile, 0.0)
    first = lower + lower.T + jnp.where(row_ids == col_ids, tile, 0.0)
    last = upper + upper.T + jnp.where(row_ids == col_ids, diagonal, 0.0)
    top = jnp.concatenate([first, cross], axis=1)
    return jnp.concatenate([top, jnp.concatenate([cross.T, last], axis=1)], axis=0)


def kernel(
    groups, members, factor_ref, support_ref, plan_ref, out_ref,
    held, cur, send, recv, acc, gram, gram_in, rot, stack,
    load_sem, store_sem, move_send, move_recv, swap_send, swap_recv, sum_send, sum_recv, rot_send, rot_recv,
):
    slots, rows, _ = cur.shape
    size = 2 * W
    chunk = rows // CHUNKS
    chips = members // 2
    stages = chips.bit_length() - 1
    g = lax.axis_index("col")
    m = lax.axis_index("row")
    core = lax.rem(m, 2)
    chip = m // 2
    partner = m + 1 - 2 * core
    half = g // 2
    goals = [2 - half, g + 1 - 2 * lax.rem(g, 2), 3 - 3 * half]

    def flipped(bit):
        step = 1 << bit
        on = lax.rem(chip // step, 2)
        return (chip + step - 2 * step * on) * 2 + core

    loads = []
    for q in range(CHUNKS):
        span = pl.ds(q * chunk, chunk)
        loads.append(pltpu.make_async_copy(factor_ref.at[span], held.at[span], load_sem.at[q]))
        loads[q].start()

    goal_peers = [{"col": goal, "row": m} for goal in goals]
    row_peers = [{"col": g, "row": partner}]
    row_peers += [{"col": g, "row": flipped(b)} for b in range(stages)]
    barrier = pltpu.get_barrier_semaphore()
    for peer in goal_peers + row_peers:
        pl.semaphore_signal(barrier, inc=1, device_id=peer, device_id_type=MESH)

    row_ids = lax.broadcasted_iota(jnp.int32, (size, size), 0)
    col_ids = lax.broadcasted_iota(jnp.int32, (size, size), 1)
    eye = (row_ids == col_ids).astype(F32)

    def mask(q):
        loads[q].wait()
        for s in range(slots):
            for b in range(q * chunk // RB, (q + 1) * chunk // RB):
                span = pl.ds(b * RB, RB)
                weight = support_ref[b, g * slots + s].astype(F32)
                cur[s, span] = held[span, s * W:(s + 1) * W] * weight

    def before(r, position):
        return position if r == 0 else plan_ref[r - 1, position]

    blocks = groups * slots
    pick, keep, take = [], [], []
    for r in range(ROUNDS):
        dest = []
        for s in range(slots):
            block = before(r, g * slots + s)
            dest.append(sum(
                jnp.where(plan_ref[r, j] == block, j // slots, 0) for j in range(blocks)))

        def slot_for(goal):
            return jnp.minimum(slots - 1, sum(
                jnp.where(dest[s] == goal, s, 0) for s in range(slots)))

        pick.append([slot_for(goal) for goal in goals])
        keep.append(slot_for(g))
        take.append([])
        for s in range(slots):
            block = plan_ref[r, g * slots + s]
            take[r].append(jnp.minimum(groups - 1, sum(
                jnp.where(before(r, j) == block, j // slots, 0) for j in range(blocks))))

    copies, stores = [], []

    def start(copy):
        copy.start()
        copies.append(copy)
        return copy

    def move(r, q, j, source):
        span = pl.ds(q * chunk, chunk)
        return pltpu.make_async_remote_copy(
            src_ref=send.at[r, j, span],
            dst_ref=recv[r][q].at[source],
            send_sem=move_send.at[r, q, j],
            recv_sem=move_recv.at[r, q, source],
            device_id=goal_peers[j],
            device_id_type=MESH,
        )

    def prepare(r, q):
        span = pl.ds(q * chunk, chunk)
        for j in range(groups - 1):
            send[r, j, span] = cur[pick[r][j], span]
        recv[r][q][g] = cur[keep[r], span]

    def arrive(r, q):
        for o in range(1, groups):
            move(r, q, 0, lax.rem(g + o, groups)).wait_recv()

    def load_pair(r, k, q):
        first = jnp.where(k == 0, take[r][0], take[r][2])
        last = jnp.where(k == 0, take[r][1], take[r][3])
        return jnp.concatenate([recv[r][q][first], recv[r][q][last]], axis=1)

    mask(0)
    prepare(0, 0)
    pl.semaphore_wait(barrier, groups - 1 + len(row_peers))
    for q in range(CHUNKS):
        if q:
            mask(q)
            prepare(0, q)
        for j in range(groups - 2):
            start(move(0, q, j, g))
    for q in range(CHUNKS):
        start(move(0, q, groups - 2, g))
    for r in range(ROUNDS):
        for q in range(CHUNKS):
            arrive(r, q)
            for k in range(2):
                high, low = split(load_pair(r, k, q))
                mixed = dot_t(high, low)
                part = dot_t(high, high) + (mixed + mixed.T)
                acc[k] = part if q == 0 else acc[k] + part
        for k in range(2):
            cross, tile, diagonal = pack(acc[k])
            gram_in[r, k, :W] = cross
            gram_in[r, k, W:size] = tile
            gram_in[r, k, size:] = diagonal
        swap = start(pltpu.make_async_remote_copy(
            src_ref=gram_in.at[r, 1 - core],
            dst_ref=gram_in.at[r, 2],
            send_sem=swap_send.at[r],
            recv_sem=swap_recv.at[r],
            device_id=row_peers[0],
            device_id_type=MESH,
        ))
        swap.wait_recv()
        total = gram_in[r, core] + gram_in[r, 2]
        for stage in range(stages):
            gram[r, 2 * stage] = total
            pair = []
            for h in range(2):
                bit = (stage + h * (stages // 2)) % stages
                part = pl.ds(0, W) if h == 0 else pl.ds(W, W + 8)
                pair.append(start(pltpu.make_async_remote_copy(
                    src_ref=gram.at[r, 2 * stage, part],
                    dst_ref=gram.at[r, 2 * stage + 1, part],
                    send_sem=sum_send.at[r, stage, h],
                    recv_sem=sum_recv.at[r, stage, h],
                    device_id=row_peers[1 + bit],
                    device_id_type=MESH,
                )))
            for copy in pair:
                copy.wait_recv()
            total = total + gram[r, 2 * stage + 1]
        rot[r, 0] = rotation(unpack(total), eye, stack)
        back = start(pltpu.make_async_remote_copy(
            src_ref=rot.at[r, 0],
            dst_ref=rot.at[r, 1],
            send_sem=rot_send.at[r],
            recv_sem=rot_recv.at[r],
            device_id=row_peers[0],
            device_id_type=MESH,
        ))
        for side in range(2):
            k = core if side == 0 else 1 - core
            if side == 1:
                back.wait_recv()
            for q in range(CHUNKS):
                span = pl.ds(q * chunk, chunk)
                turned = dot3(load_pair(r, k, q), rot[r, side])
                if r == ROUNDS - 1:
                    lanes = pl.ds(pl.multiple_of(k * size, size), size)
                    held[span, lanes] = turned
                    stores.append(pltpu.make_async_copy(
                        held.at[span, lanes], out_ref.at[span, lanes], store_sem.at[side, q]))
                    stores[-1].start()
                else:
                    cur[2 * k, span] = turned[:, :W]
                    cur[2 * k + 1, span] = turned[:, W:]
                    if side == 1:
                        prepare(r + 1, q)
                        for j in range(groups - 1):
                            start(move(r + 1, q, j, g))
    for copy in copies:
        copy.wait_send()
    for copy in stores:
        copy.wait()


def on_device(groups, members, factor, support, plan):
    rows = factor.shape[0]
    slots = factor.shape[1] // W
    chips = members // 2
    stages = chips.bit_length() - 1
    assert slots == 4 and groups == 4 and chips == 1 << stages and stages >= 1 and ROUNDS == 2
    size = 2 * W
    dma = pltpu.SemaphoreType.DMA
    smem = pl.BlockSpec(memory_space=pltpu.SMEM)
    return pl.pallas_call(
        functools.partial(kernel, groups, members),
        out_shape=jax.ShapeDtypeStruct(factor.shape, F32),
        in_specs=[pl.BlockSpec(memory_space=pl.ANY), smem, smem],
        out_specs=pl.BlockSpec(memory_space=pl.ANY),
        scratch_shapes=[
            pltpu.VMEM(factor.shape, F32),
            pltpu.VMEM((slots, rows, W), F32),
            pltpu.VMEM((ROUNDS, groups - 1, rows, W), F32),
            [[pltpu.VMEM((groups, rows // CHUNKS, W), F32)] * CHUNKS] * ROUNDS,
            pltpu.VMEM((2, size, size), F32),
            pltpu.VMEM((ROUNDS, 2 * stages, size + 8, W), F32),
            pltpu.VMEM((ROUNDS, 3, size + 8, W), F32),
            pltpu.VMEM((ROUNDS, 2, size, size), F32),
            pltpu.VMEM((2 * size, size), F32),
            dma((CHUNKS,)),
            dma((2, CHUNKS)),
            dma((ROUNDS, CHUNKS, groups - 1)),
            dma((ROUNDS, CHUNKS, groups)),
            dma((ROUNDS,)),
            dma((ROUNDS,)),
            dma((ROUNDS, stages, 2)),
            dma((ROUNDS, stages, 2)),
            dma((ROUNDS,)),
            dma((ROUNDS,)),
        ],
        compiler_params=pltpu.CompilerParams(
            collective_id=0, has_side_effects=True, vmem_limit_bytes=123 * 512 * 1024
        ),
    )(factor, support.T, plan)


def solution(mesh):
    return jax.shard_map(
        functools.partial(on_device, mesh.shape["col"], mesh.shape["row"]),
        mesh=mesh,
        in_specs=(P("row", "col"), P(None, "row"), P()),
        out_specs=P("row", "col"),
        check_vma=False,
    )
```

```python
import functools

import jax
import jax.numpy as jnp
from jax import lax
from jax.experimental import pallas as pl
from jax.experimental.pallas import tpu as pltpu
from jax.sharding import PartitionSpec as P

W = 128
RB = 128
ROUNDS = 2
CHUNKS = 4
SCALED_STEPS = 7
TRUE_STEPS = 2
DAMPING = 0.01
F32 = jnp.float32
BF16 = jnp.bfloat16
MESH = pl.DeviceIdType.MESH


def split(x):
    high = x.astype(BF16)
    return high, (x - high.astype(F32)).astype(BF16)


def dot(a, b):
    return jnp.dot(a, b, preferred_element_type=F32)


def dot3(a, b):
    a_high, a_low = split(a)
    b_high, b_low = split(b)
    return dot(a_high, b_high) + (dot(a_high, b_low) + dot(a_low, b_high))


def dot_t(a, b):
    return lax.dot_general(a, b, (((0,), (0,)), ((), ())), preferred_element_type=F32)


def rotation(gram, eye, stack):
    size = gram.shape[0]
    on_diagonal = gram * eye
    diag_rows = jnp.sum(on_diagonal, axis=1, keepdims=True)
    diag_cols = jnp.sum(on_diagonal, axis=0, keepdims=True)
    spread = diag_rows - diag_cols
    joined = diag_rows + diag_cols
    half = 0.5 * gram * spread / (spread * spread + gram * gram + DAMPING * joined * joined)
    squared = dot3(half, half)
    total = jnp.sum(jnp.sum(squared * squared, axis=1, keepdims=True), axis=0, keepdims=True)
    upper = 1.0 + 1.001 * jnp.sqrt(0.5 * total)
    stack[:size] = eye - squared
    stack[size:] = eye - half

    def scaled(_, bounds):
        low, high = bounds
        scale = 2.0 / (low + high)
        delta = (high - low) / (high + low)
        factor = (2.0 * scale) * eye - (scale * scale) * stack[:size]
        stack[...] = dot3(stack[...], factor)
        return 1.0 - delta * delta, jnp.ones_like(high)

    lax.fori_loop(0, SCALED_STEPS, scaled, (jnp.ones_like(upper), upper))

    def true(_, carry):
        inverse = stack[size:]
        residual = (eye - inverse) - dot3(half, inverse)
        stack[size:] = inverse + dot3(inverse, residual)
        return carry

    lax.fori_loop(0, TRUE_STEPS, true, 0)
    return 2.0 * stack[size:] - eye


def pack(gram):
    first, last = gram[:W, :W], gram[W:, W:]
    row_ids = lax.broadcasted_iota(jnp.int32, (W, W), 0)
    col_ids = lax.broadcasted_iota(jnp.int32, (W, W), 1)
    tile = jnp.where(row_ids >= col_ids, first, last)
    diagonal = jnp.sum(jnp.where(row_ids == col_ids, last, 0.0), axis=0, keepdims=True)
    return gram[:W, W:], tile, jnp.broadcast_to(diagonal, (8, W))


def unpack(packed):
    cross, tile, diagonal = packed[:W], packed[W:2 * W], packed[2 * W:2 * W + 1]
    row_ids = lax.broadcasted_iota(jnp.int32, (W, W), 0)
    col_ids = lax.broadcasted_iota(jnp.int32, (W, W), 1)
    lower = jnp.where(row_ids > col_ids, tile, 0.0)
    upper = jnp.where(row_ids < col_ids, tile, 0.0)
    first = lower + lower.T + jnp.where(row_ids == col_ids, tile, 0.0)
    last = upper + upper.T + jnp.where(row_ids == col_ids, diagonal, 0.0)
    top = jnp.concatenate([first, cross], axis=1)
    return jnp.concatenate([top, jnp.concatenate([cross.T, last], axis=1)], axis=0)


def kernel(
    groups, members, factor_ref, support_ref, plan_ref, out_ref,
    held, cur, send, recv, raw_out, raw_in, turn_out, turn, acc, gram, gram_in, rot, stack,
    load_sem, store_sem, move_send, move_recv, raw_send, raw_recv, turn_send, turn_recv, swap_send, swap_recv, sum_send, sum_recv, rot_send, rot_recv,
):
    slots, rows, _ = cur.shape
    size = 2 * W
    chunk = rows // CHUNKS
    chips = members // 2
    stages = chips.bit_length() - 1
    g = lax.axis_index("col")
    m = lax.axis_index("row")
    core = lax.rem(m, 2)
    chip = m // 2
    partner = m + 1 - 2 * core
    half = g // 2
    at_end = jnp.logical_or(g == 0, g == groups - 1)
    inside = jnp.logical_not(at_end)
    goals = [2 - half, g + 1 - 2 * lax.rem(g, 2), 3 - 3 * half]

    def flipped(bit):
        step = 1 << bit
        on = lax.rem(chip // step, 2)
        return (chip + step - 2 * step * on) * 2 + core

    loads = []
    for q in range(CHUNKS):
        span = pl.ds(q * chunk, chunk)
        loads.append(pltpu.make_async_copy(factor_ref.at[span], held.at[span], load_sem.at[q]))
        loads[q].start()

    goal_peers = [{"col": goal, "row": m} for goal in goals]
    row_peers = [{"col": g, "row": partner}]
    row_peers += [{"col": g, "row": flipped(b)} for b in range(stages)]
    barrier = pltpu.get_barrier_semaphore()
    for peer in goal_peers + row_peers:
        pl.semaphore_signal(barrier, inc=1, device_id=peer, device_id_type=MESH)

    row_ids = lax.broadcasted_iota(jnp.int32, (size, size), 0)
    col_ids = lax.broadcasted_iota(jnp.int32, (size, size), 1)
    eye = (row_ids == col_ids).astype(F32)

    def mask(q):
        loads[q].wait()
        for s in range(slots):
            for b in range(q * chunk // RB, (q + 1) * chunk // RB):
                span = pl.ds(b * RB, RB)
                weight = support_ref[b, g * slots + s].astype(F32)
                cur[s, span] = held[span, s * W:(s + 1) * W] * weight

    def before(r, position):
        return position if r == 0 else plan_ref[r - 1, position]

    blocks = groups * slots
    pick, keep, take = [], [], []
    for r in range(ROUNDS):
        dest = []
        for s in range(slots):
            block = before(r, g * slots + s)
            dest.append(sum(
                jnp.where(plan_ref[r, j] == block, j // slots, 0) for j in range(blocks)))

        def slot_for(goal):
            return jnp.minimum(slots - 1, sum(
                jnp.where(dest[s] == goal, s, 0) for s in range(slots)))

        pick.append([slot_for(goal) for goal in goals])
        keep.append(slot_for(g))
        take.append([])
        for s in range(slots):
            block = plan_ref[r, g * slots + s]
            take[r].append(jnp.minimum(groups - 1, sum(
                jnp.where(before(r, j) == block, j // slots, 0) for j in range(blocks))))

    copies, stores = [], []

    def start(copy):
        copy.start()
        copies.append(copy)
        return copy

    def move(r, q, j, source):
        span = pl.ds(q * chunk, chunk)
        return pltpu.make_async_remote_copy(
            src_ref=send.at[r, j, span],
            dst_ref=recv[r][q].at[source],
            send_sem=move_send.at[r, q, j],
            recv_sem=move_recv.at[r, q, source],
            device_id=goal_peers[j],
            device_id_type=MESH,
        )

    def prepare(r, q):
        span = pl.ds(q * chunk, chunk)
        for j in range(groups - 1):
            send[r, j, span] = cur[pick[r][j], span]
        recv[r][q][g] = cur[keep[r], span]

    def arrive(r, q):
        for s in range(2):
            move(r, q, 0, 2 - 2 * half + s).wait_recv()
        if r == 0:
            move(r, q, 0, goals[1]).wait_recv()
        else:
            @pl.when(at_end)
            def _():
                move(r, q, 0, goals[1]).wait_recv()

    raws = [pltpu.make_async_remote_copy(
        src_ref=raw_out.at[q],
        dst_ref=raw_in.at[q],
        send_sem=raw_send.at[q],
        recv_sem=raw_recv.at[q],
        device_id=goal_peers[1],
        device_id_type=MESH,
    ) for q in range(CHUNKS)]
    near_slot = pick[1][1]
    share = pl.ds(pl.multiple_of(core * W, W), W)
    turn_copy = pltpu.make_async_remote_copy(
        src_ref=turn_out,
        dst_ref=turn.at[share],
        send_sem=turn_send.at[0],
        recv_sem=turn_recv.at[0],
        device_id=goal_peers[1],
        device_id_type=MESH,
    )
    turn_swap = pltpu.make_async_remote_copy(
        src_ref=turn.at[share],
        dst_ref=turn.at[share],
        send_sem=turn_send.at[1],
        recv_sem=turn_recv.at[1],
        device_id=row_peers[0],
        device_id_type=MESH,
    )

    def start_raw(q):
        @pl.when(at_end)
        def _():
            raw_out[q] = load_pair(0, near_slot // 2, q)
            raws[q].start()

    def start_turn():
        @pl.when(at_end)
        def _():
            side = jnp.where(near_slot // 2 == core, 0, 1)
            wide = rot[0, side, share]
            turn_out[...] = jnp.where(lax.rem(near_slot, 2) == 0, wide[:, :W], wide[:, W:])
            turn_copy.start()

    def turn_raws():
        @pl.when(inside)
        def _():
            turn_copy.wait_recv()
            turn_swap.start()
            turn_swap.wait_recv()
            for q in range(CHUNKS):
                raws[q].wait_recv()
                recv[1][q][goals[1]] = dot3(raw_in[q], turn[...])

    def start_near(q):
        @pl.when(inside)
        def _():
            move(1, q, 1, g).start()

    def load_pair(r, k, q):
        first = jnp.where(k == 0, take[r][0], take[r][2])
        last = jnp.where(k == 0, take[r][1], take[r][3])
        return jnp.concatenate([recv[r][q][first], recv[r][q][last]], axis=1)

    mask(0)
    prepare(0, 0)
    pl.semaphore_wait(barrier, groups - 1 + len(row_peers))
    for q in range(CHUNKS):
        if q:
            mask(q)
            prepare(0, q)
        for j in range(groups - 2):
            start(move(0, q, j, g))
    for q in range(CHUNKS):
        start(move(0, q, groups - 2, g))
    for r in range(ROUNDS):
        if r == 1:
            turn_raws()
        for q in range(CHUNKS):
            arrive(r, q)
            if r == 0:
                start_raw(q)
            for k in range(2):
                high, low = split(load_pair(r, k, q))
                mixed = dot_t(high, low)
                part = dot_t(high, high) + (mixed + mixed.T)
                acc[k] = part if q == 0 else acc[k] + part
        for k in range(2):
            cross, tile, diagonal = pack(acc[k])
            gram_in[r, k, :W] = cross
            gram_in[r, k, W:size] = tile
            gram_in[r, k, size:] = diagonal
        swap = start(pltpu.make_async_remote_copy(
            src_ref=gram_in.at[r, 1 - core],
            dst_ref=gram_in.at[r, 2],
            send_sem=swap_send.at[r],
            recv_sem=swap_recv.at[r],
            device_id=row_peers[0],
            device_id_type=MESH,
        ))
        swap.wait_recv()
        total = gram_in[r, core] + gram_in[r, 2]
        for stage in range(stages):
            gram[r, 2 * stage] = total
            pair = []
            for h in range(2):
                bit = (stage + h * (stages // 2)) % stages
                part = pl.ds(0, W) if h == 0 else pl.ds(W, W + 8)
                pair.append(start(pltpu.make_async_remote_copy(
                    src_ref=gram.at[r, 2 * stage, part],
                    dst_ref=gram.at[r, 2 * stage + 1, part],
                    send_sem=sum_send.at[r, stage, h],
                    recv_sem=sum_recv.at[r, stage, h],
                    device_id=row_peers[1 + bit],
                    device_id_type=MESH,
                )))
            for copy in pair:
                copy.wait_recv()
            total = total + gram[r, 2 * stage + 1]
        rot[r, 0] = rotation(unpack(total), eye, stack)
        back = start(pltpu.make_async_remote_copy(
            src_ref=rot.at[r, 0],
            dst_ref=rot.at[r, 1],
            send_sem=rot_send.at[r],
            recv_sem=rot_recv.at[r],
            device_id=row_peers[0],
            device_id_type=MESH,
        ))
        for side in range(2):
            k = core if side == 0 else 1 - core
            if side == 1:
                back.wait_recv()
            if side == 1 and r == 0:
                start_turn()
            for q in range(CHUNKS):
                span = pl.ds(q * chunk, chunk)
                turned = dot3(load_pair(r, k, q), rot[r, side])
                if r == ROUNDS - 1:
                    lanes = pl.ds(pl.multiple_of(k * size, size), size)
                    held[span, lanes] = turned
                    stores.append(pltpu.make_async_copy(
                        held.at[span, lanes], out_ref.at[span, lanes], store_sem.at[side, q]))
                    stores[-1].start()
                else:
                    cur[2 * k, span] = turned[:, :W]
                    cur[2 * k + 1, span] = turned[:, W:]
                    if side == 1:
                        prepare(r + 1, q)
                        for j in (0, groups - 2):
                            start(move(r + 1, q, j, g))
                        start_near(q)
    @pl.when(at_end)
    def _():
        for copy in [*raws, turn_copy]:
            copy.wait_send()

    @pl.when(inside)
    def _():
        turn_swap.wait_send()
        for q in range(CHUNKS):
            move(1, q, 1, g).wait_send()

    for copy in copies:
        copy.wait_send()
    for copy in stores:
        copy.wait()


def on_device(groups, members, factor, support, plan):
    rows = factor.shape[0]
    slots = factor.shape[1] // W
    chips = members // 2
    stages = chips.bit_length() - 1
    assert slots == 4 and groups == 4 and chips == 1 << stages and stages >= 1 and ROUNDS == 2
    size = 2 * W
    dma = pltpu.SemaphoreType.DMA
    smem = pl.BlockSpec(memory_space=pltpu.SMEM)
    return pl.pallas_call(
        functools.partial(kernel, groups, members),
        out_shape=jax.ShapeDtypeStruct(factor.shape, F32),
        in_specs=[pl.BlockSpec(memory_space=pl.ANY), smem, smem],
        out_specs=pl.BlockSpec(memory_space=pl.ANY),
        scratch_shapes=[
            pltpu.VMEM(factor.shape, F32),
            pltpu.VMEM((slots, rows, W), F32),
            pltpu.VMEM((ROUNDS, groups - 1, rows, W), F32),
            [[pltpu.VMEM((groups, rows // CHUNKS, W), F32)] * CHUNKS] * ROUNDS,
            pltpu.VMEM((CHUNKS, rows // CHUNKS, size), F32),
            pltpu.VMEM((CHUNKS, rows // CHUNKS, size), F32),
            pltpu.VMEM((W, W), F32),
            pltpu.VMEM((size, W), F32),
            pltpu.VMEM((2, size, size), F32),
            pltpu.VMEM((ROUNDS, 2 * stages, size + 8, W), F32),
            pltpu.VMEM((ROUNDS, 3, size + 8, W), F32),
            pltpu.VMEM((ROUNDS, 2, size, size), F32),
            pltpu.VMEM((2 * size, size), F32),
            dma((CHUNKS,)),
            dma((2, CHUNKS)),
            dma((ROUNDS, CHUNKS, groups - 1)),
            dma((ROUNDS, CHUNKS, groups)),
            dma((CHUNKS,)),
            dma((CHUNKS,)),
            dma((2,)),
            dma((2,)),
            dma((ROUNDS,)),
            dma((ROUNDS,)),
            dma((ROUNDS, stages, 2)),
            dma((ROUNDS, stages, 2)),
            dma((ROUNDS,)),
            dma((ROUNDS,)),
        ],
        compiler_params=pltpu.CompilerParams(
            collective_id=0, has_side_effects=True, vmem_limit_bytes=123 * 512 * 1024
        ),
    )(factor, support.T, plan)


def solution(mesh):
    return jax.shard_map(
        functools.partial(on_device, mesh.shape["col"], mesh.shape["row"]),
        mesh=mesh,
        in_specs=(P("row", "col"), P(None, "row"), P()),
        out_specs=P("row", "col"),
        check_vma=False,
    )
```

```python
import functools

import jax
import jax.numpy as jnp
from jax import lax
from jax.experimental import pallas as pl
from jax.experimental.pallas import tpu as pltpu
from jax.sharding import PartitionSpec as P

W = 128
RB = 128
ROUNDS = 2
CHUNKS = 4
SCALED_STEPS = 7
TRUE_STEPS = 2
DAMPING = 0.01
F32 = jnp.float32
BF16 = jnp.bfloat16
MESH = pl.DeviceIdType.MESH


def split(x):
    high = x.astype(BF16)
    return high, (x - high.astype(F32)).astype(BF16)


def dot(a, b):
    return jnp.dot(a, b, preferred_element_type=F32)


def dot3(a, b):
    a_high, a_low = split(a)
    b_high, b_low = split(b)
    return dot(a_high, b_high) + (dot(a_high, b_low) + dot(a_low, b_high))


def dot_t(a, b):
    return lax.dot_general(a, b, (((0,), (0,)), ((), ())), preferred_element_type=F32)


def rotation(gram, eye, stack):
    size = gram.shape[0]
    on_diagonal = gram * eye
    diag_rows = jnp.sum(on_diagonal, axis=1, keepdims=True)
    diag_cols = jnp.sum(on_diagonal, axis=0, keepdims=True)
    spread = diag_rows - diag_cols
    joined = diag_rows + diag_cols
    half = 0.5 * gram * spread / (spread * spread + gram * gram + DAMPING * joined * joined)
    squared = dot3(half, half)
    total = jnp.sum(jnp.sum(squared * squared, axis=1, keepdims=True), axis=0, keepdims=True)
    upper = 1.0 + 1.001 * jnp.sqrt(0.5 * total)
    stack[:size] = eye - squared
    stack[size:] = eye - half

    def scaled(_, bounds):
        low, high = bounds
        scale = 2.0 / (low + high)
        delta = (high - low) / (high + low)
        factor = (2.0 * scale) * eye - (scale * scale) * stack[:size]
        stack[...] = dot3(stack[...], factor)
        return 1.0 - delta * delta, jnp.ones_like(high)

    lax.fori_loop(0, SCALED_STEPS, scaled, (jnp.ones_like(upper), upper))

    def true(_, carry):
        inverse = stack[size:]
        residual = (eye - inverse) - dot3(half, inverse)
        stack[size:] = inverse + dot3(inverse, residual)
        return carry

    lax.fori_loop(0, TRUE_STEPS, true, 0)
    return 2.0 * stack[size:] - eye


def pack(gram):
    first, last = gram[:W, :W], gram[W:, W:]
    row_ids = lax.broadcasted_iota(jnp.int32, (W, W), 0)
    col_ids = lax.broadcasted_iota(jnp.int32, (W, W), 1)
    tile = jnp.where(row_ids >= col_ids, first, last)
    diagonal = jnp.sum(jnp.where(row_ids == col_ids, last, 0.0), axis=0, keepdims=True)
    return gram[:W, W:], tile, jnp.broadcast_to(diagonal, (8, W))


def unpack(packed):
    cross, tile, diagonal = packed[:W], packed[W:2 * W], packed[2 * W:2 * W + 1]
    row_ids = lax.broadcasted_iota(jnp.int32, (W, W), 0)
    col_ids = lax.broadcasted_iota(jnp.int32, (W, W), 1)
    lower = jnp.where(row_ids > col_ids, tile, 0.0)
    upper = jnp.where(row_ids < col_ids, tile, 0.0)
    first = lower + lower.T + jnp.where(row_ids == col_ids, tile, 0.0)
    last = upper + upper.T + jnp.where(row_ids == col_ids, diagonal, 0.0)
    top = jnp.concatenate([first, cross], axis=1)
    return jnp.concatenate([top, jnp.concatenate([cross.T, last], axis=1)], axis=0)


def kernel(
    groups, members, factor_ref, support_ref, plan_ref, out_ref,
    held, cur, send, recv, raw_out, raw_in, turn_out, turn, acc, gram, gram_in, rot, stack,
    load_sem, move_send, move_recv, raw_send, raw_recv, turn_send, turn_recv, swap_send, swap_recv, sum_send, sum_recv, rot_send, rot_recv,
):
    slots, rows, _ = cur.shape
    size = 2 * W
    chunk = rows // CHUNKS
    chips = members // 2
    stages = chips.bit_length() - 1
    g = lax.axis_index("col")
    m = lax.axis_index("row")
    core = lax.rem(m, 2)
    chip = m // 2
    partner = m + 1 - 2 * core
    half = g // 2
    at_end = jnp.logical_or(g == 0, g == groups - 1)
    inside = jnp.logical_not(at_end)
    goals = [2 - half, g + 1 - 2 * lax.rem(g, 2), 3 - 3 * half]

    def flipped(bit):
        step = 1 << bit
        on = lax.rem(chip // step, 2)
        return (chip + step - 2 * step * on) * 2 + core

    loads = []
    for q in range(CHUNKS):
        span = pl.ds(q * chunk, chunk)
        loads.append(pltpu.make_async_copy(factor_ref.at[span], held.at[span], load_sem.at[q]))
        loads[q].start()

    goal_peers = [{"col": goal, "row": m} for goal in goals]
    row_peers = [{"col": g, "row": partner}]
    row_peers += [{"col": g, "row": flipped(b)} for b in range(stages)]
    barrier = pltpu.get_barrier_semaphore()
    for peer in goal_peers + row_peers:
        pl.semaphore_signal(barrier, inc=1, device_id=peer, device_id_type=MESH)

    row_ids = lax.broadcasted_iota(jnp.int32, (size, size), 0)
    col_ids = lax.broadcasted_iota(jnp.int32, (size, size), 1)
    eye = (row_ids == col_ids).astype(F32)

    def mask(q):
        loads[q].wait()
        for s in range(slots):
            for b in range(q * chunk // RB, (q + 1) * chunk // RB):
                span = pl.ds(b * RB, RB)
                weight = support_ref[b, g * slots + s].astype(F32)
                cur[s, span] = held[span, s * W:(s + 1) * W] * weight

    def before(r, position):
        return position if r == 0 else plan_ref[r - 1, position]

    blocks = groups * slots
    pick, keep, take = [], [], []
    for r in range(ROUNDS):
        dest = []
        for s in range(slots):
            block = before(r, g * slots + s)
            dest.append(sum(
                jnp.where(plan_ref[r, j] == block, j // slots, 0) for j in range(blocks)))

        def slot_for(goal):
            return jnp.minimum(slots - 1, sum(
                jnp.where(dest[s] == goal, s, 0) for s in range(slots)))

        pick.append([slot_for(goal) for goal in goals])
        keep.append(slot_for(g))
        take.append([])
        for s in range(slots):
            block = plan_ref[r, g * slots + s]
            take[r].append(jnp.minimum(groups - 1, sum(
                jnp.where(before(r, j) == block, j // slots, 0) for j in range(blocks))))

    copies = []

    def start(copy):
        copy.start()
        copies.append(copy)
        return copy

    def move(r, q, j, source):
        span = pl.ds(q * chunk, chunk)
        return pltpu.make_async_remote_copy(
            src_ref=send.at[r, j, span],
            dst_ref=recv[r][q].at[source],
            send_sem=move_send.at[r, q, j],
            recv_sem=move_recv.at[r, q, source],
            device_id=goal_peers[j],
            device_id_type=MESH,
        )

    def prepare(r, q):
        span = pl.ds(q * chunk, chunk)
        for j in range(groups - 1):
            send[r, j, span] = cur[pick[r][j], span]
        recv[r][q][g] = cur[keep[r], span]

    def arrive(r, q):
        for s in range(2):
            move(r, q, 0, 2 - 2 * half + s).wait_recv()
        if r == 0:
            move(r, q, 0, goals[1]).wait_recv()
        else:
            @pl.when(at_end)
            def _():
                move(r, q, 0, goals[1]).wait_recv()

    raws = [pltpu.make_async_remote_copy(
        src_ref=raw_out.at[q],
        dst_ref=raw_in.at[q],
        send_sem=raw_send.at[q],
        recv_sem=raw_recv.at[q],
        device_id=goal_peers[1],
        device_id_type=MESH,
    ) for q in range(CHUNKS)]
    near_slot = pick[1][1]
    share = pl.ds(pl.multiple_of(core * W, W), W)
    turn_copy = pltpu.make_async_remote_copy(
        src_ref=turn_out,
        dst_ref=turn.at[share],
        send_sem=turn_send.at[0],
        recv_sem=turn_recv.at[0],
        device_id=goal_peers[1],
        device_id_type=MESH,
    )
    turn_swap = pltpu.make_async_remote_copy(
        src_ref=turn.at[share],
        dst_ref=turn.at[share],
        send_sem=turn_send.at[1],
        recv_sem=turn_recv.at[1],
        device_id=row_peers[0],
        device_id_type=MESH,
    )

    def start_raw(q):
        @pl.when(at_end)
        def _():
            raw_out[q] = load_pair(0, near_slot // 2, q)
            raws[q].start()

    def start_turn():
        @pl.when(at_end)
        def _():
            side = jnp.where(near_slot // 2 == core, 0, 1)
            wide = rot[0, side, share]
            turn_out[...] = jnp.where(lax.rem(near_slot, 2) == 0, wide[:, :W], wide[:, W:])
            turn_copy.start()

    def turn_raws():
        @pl.when(inside)
        def _():
            turn_copy.wait_recv()
            turn_swap.start()
            turn_swap.wait_recv()
            for q in range(CHUNKS):
                raws[q].wait_recv()
                recv[1][q][goals[1]] = dot3(raw_in[q], turn[...])

    def start_near(q):
        @pl.when(inside)
        def _():
            move(1, q, 1, g).start()

    def load_pair(r, k, q):
        first = jnp.where(k == 0, take[r][0], take[r][2])
        last = jnp.where(k == 0, take[r][1], take[r][3])
        return jnp.concatenate([recv[r][q][first], recv[r][q][last]], axis=1)

    mask(0)
    prepare(0, 0)
    pl.semaphore_wait(barrier, groups - 1 + len(row_peers))
    for q in range(CHUNKS):
        if q:
            mask(q)
            prepare(0, q)
        for j in range(groups - 2):
            start(move(0, q, j, g))
    for q in range(CHUNKS):
        start(move(0, q, groups - 2, g))
    for r in range(ROUNDS):
        if r == 1:
            turn_raws()
        for q in range(CHUNKS):
            arrive(r, q)
            if r == 0:
                start_raw(q)
            for k in range(2):
                high, low = split(load_pair(r, k, q))
                mixed = dot_t(high, low)
                part = dot_t(high, high) + (mixed + mixed.T)
                acc[k] = part if q == 0 else acc[k] + part
        for k in range(2):
            cross, tile, diagonal = pack(acc[k])
            gram_in[r, k, :W] = cross
            gram_in[r, k, W:size] = tile
            gram_in[r, k, size:] = diagonal
        swap = start(pltpu.make_async_remote_copy(
            src_ref=gram_in.at[r, 1 - core],
            dst_ref=gram_in.at[r, 2],
            send_sem=swap_send.at[r],
            recv_sem=swap_recv.at[r],
            device_id=row_peers[0],
            device_id_type=MESH,
        ))
        swap.wait_recv()
        total = gram_in[r, core] + gram_in[r, 2]
        for stage in range(stages):
            gram[r, 2 * stage] = total
            pair = []
            for h in range(2):
                bit = (stage + h * (stages // 2)) % stages
                part = pl.ds(0, W) if h == 0 else pl.ds(W, W + 8)
                pair.append(start(pltpu.make_async_remote_copy(
                    src_ref=gram.at[r, 2 * stage, part],
                    dst_ref=gram.at[r, 2 * stage + 1, part],
                    send_sem=sum_send.at[r, stage, h],
                    recv_sem=sum_recv.at[r, stage, h],
                    device_id=row_peers[1 + bit],
                    device_id_type=MESH,
                )))
            for copy in pair:
                copy.wait_recv()
            total = total + gram[r, 2 * stage + 1]
        rot[r, 0] = rotation(unpack(total), eye, stack)
        back = start(pltpu.make_async_remote_copy(
            src_ref=rot.at[r, 0],
            dst_ref=rot.at[r, 1],
            send_sem=rot_send.at[r],
            recv_sem=rot_recv.at[r],
            device_id=row_peers[0],
            device_id_type=MESH,
        ))
        for side in range(2):
            k = core if side == 0 else 1 - core
            if side == 1:
                back.wait_recv()
            if side == 1 and r == 0:
                start_turn()
            for q in range(CHUNKS):
                span = pl.ds(q * chunk, chunk)
                turned = dot3(load_pair(r, k, q), rot[r, side])
                if r == ROUNDS - 1:
                    lanes = pl.ds(pl.multiple_of(k * size, size), size)
                    out_ref[span, lanes] = turned
                else:
                    cur[2 * k, span] = turned[:, :W]
                    cur[2 * k + 1, span] = turned[:, W:]
                    if side == 1:
                        prepare(r + 1, q)
                        for j in (0, groups - 2):
                            start(move(r + 1, q, j, g))
                        start_near(q)
    @pl.when(at_end)
    def _():
        for copy in [*raws, turn_copy]:
            copy.wait_send()

    @pl.when(inside)
    def _():
        turn_swap.wait_send()
        for q in range(CHUNKS):
            move(1, q, 1, g).wait_send()

    for copy in copies:
        copy.wait_send()


def on_device(groups, members, factor, support, plan):
    rows = factor.shape[0]
    slots = factor.shape[1] // W
    chips = members // 2
    stages = chips.bit_length() - 1
    assert slots == 4 and groups == 4 and chips == 1 << stages and stages >= 1 and ROUNDS == 2
    size = 2 * W
    dma = pltpu.SemaphoreType.DMA
    smem = pl.BlockSpec(memory_space=pltpu.SMEM)
    return pl.pallas_call(
        functools.partial(kernel, groups, members),
        out_shape=jax.ShapeDtypeStruct(factor.shape, F32),
        in_specs=[pl.BlockSpec(memory_space=pl.ANY), smem, smem],
        out_specs=pl.BlockSpec(memory_space=pltpu.VMEM),
        scratch_shapes=[
            pltpu.VMEM(factor.shape, F32),
            pltpu.VMEM((slots, rows, W), F32),
            pltpu.VMEM((ROUNDS, groups - 1, rows, W), F32),
            [[pltpu.VMEM((groups, rows // CHUNKS, W), F32)] * CHUNKS] * ROUNDS,
            pltpu.VMEM((CHUNKS, rows // CHUNKS, size), F32),
            pltpu.VMEM((CHUNKS, rows // CHUNKS, size), F32),
            pltpu.VMEM((W, W), F32),
            pltpu.VMEM((size, W), F32),
            pltpu.VMEM((2, size, size), F32),
            pltpu.VMEM((ROUNDS, 2 * stages, size + 8, W), F32),
            pltpu.VMEM((ROUNDS, 3, size + 8, W), F32),
            pltpu.VMEM((ROUNDS, 2, size, size), F32),
            pltpu.VMEM((2 * size, size), F32),
            dma((CHUNKS,)),
            dma((ROUNDS, CHUNKS, groups - 1)),
            dma((ROUNDS, CHUNKS, groups)),
            dma((CHUNKS,)),
            dma((CHUNKS,)),
            dma((2,)),
            dma((2,)),
            dma((ROUNDS,)),
            dma((ROUNDS,)),
            dma((ROUNDS, stages, 2)),
            dma((ROUNDS, stages, 2)),
            dma((ROUNDS,)),
            dma((ROUNDS,)),
        ],
        compiler_params=pltpu.CompilerParams(
            collective_id=0, has_side_effects=True, vmem_limit_bytes=30 * 1024 * 1024
        ),
    )(*(pltpu.with_memory_space_constraint(x, pltpu.HBM) for x in (factor, support.T, plan)))


def solution(mesh):
    return jax.shard_map(
        functools.partial(on_device, mesh.shape["col"], mesh.shape["row"]),
        mesh=mesh,
        in_specs=(P("row", "col"), P(None, "row"), P()),
        out_specs=P("row", "col"),
        check_vma=False,
    )
```

```python
import functools

import jax
import jax.numpy as jnp
from jax import lax
from jax.experimental import pallas as pl
from jax.experimental.pallas import tpu as pltpu
from jax.sharding import PartitionSpec as P

W = 128
RB = 128
ROUNDS = 2
CHUNKS = 4
STEPS = 7
DAMPING = 0.01
TOP = 2020.0
F32 = jnp.float32
BF16 = jnp.bfloat16
MESH = pl.DeviceIdType.MESH


def split(x):
    high = x.astype(BF16)
    return high, (x - high.astype(F32)).astype(BF16)


def dot(a, b):
    return jnp.dot(a, b, preferred_element_type=F32)


def dot3(a, b):
    a_high, a_low = split(a)
    b_high, b_low = split(b)
    return dot(a_high, b_high) + (dot(a_high, b_low) + dot(a_low, b_high))


def dot_t(a, b):
    return lax.dot_general(a, b, (((0,), (0,)), ((), ())), preferred_element_type=F32)


def rotation(gram, eye, stack):
    size = gram.shape[0]
    on_diagonal = gram * eye
    diag_rows = jnp.sum(on_diagonal, axis=1, keepdims=True)
    diag_cols = jnp.sum(on_diagonal, axis=0, keepdims=True)
    spread = diag_rows - diag_cols
    joined = diag_rows + diag_cols
    half = 0.5 * gram * spread / (spread * spread + gram * gram + DAMPING * joined * joined)
    squared = dot3(half, half)
    stack[:size] = eye - squared
    stack[size:] = eye - half
    scales, low, high = [], 1.0, TOP
    for _ in range(STEPS):
        scales.append(2.0 / (low + high))
        low, high = 4.0 * low * high / (low + high) ** 2, 1.0

    def factor(scale):
        return (2.0 * scale) * eye - (scale * scale) * stack[:size]

    def scaled(step, carry):
        scale = jnp.float32(scales[0])
        for i in range(1, STEPS - 1):
            scale = jnp.where(step == i, scales[i], scale)
        stack[...] = dot3(stack[...], factor(scale))
        return carry

    lax.fori_loop(0, STEPS - 1, scaled, 0)
    inverse = dot3(stack[size:], factor(scales[-1]))
    residual = (eye - inverse) - dot3(half, inverse)
    short = residual.astype(BF16)
    inverse = inverse + dot3(inverse, residual + dot(short, short))
    return 2.0 * inverse - eye


def pack(gram):
    first, last = gram[:W, :W], gram[W:, W:]
    row_ids = lax.broadcasted_iota(jnp.int32, (W, W), 0)
    col_ids = lax.broadcasted_iota(jnp.int32, (W, W), 1)
    tile = jnp.where(row_ids >= col_ids, first, last)
    diagonal = jnp.sum(jnp.where(row_ids == col_ids, last, 0.0), axis=0, keepdims=True)
    return gram[:W, W:], tile, jnp.broadcast_to(diagonal, (8, W))


def unpack(packed):
    cross, tile, diagonal = packed[:W], packed[W:2 * W], packed[2 * W:2 * W + 1]
    row_ids = lax.broadcasted_iota(jnp.int32, (W, W), 0)
    col_ids = lax.broadcasted_iota(jnp.int32, (W, W), 1)
    lower = jnp.where(row_ids > col_ids, tile, 0.0)
    upper = jnp.where(row_ids < col_ids, tile, 0.0)
    first = lower + lower.T + jnp.where(row_ids == col_ids, tile, 0.0)
    last = upper + upper.T + jnp.where(row_ids == col_ids, diagonal, 0.0)
    top = jnp.concatenate([first, cross], axis=1)
    return jnp.concatenate([top, jnp.concatenate([cross.T, last], axis=1)], axis=0)


def kernel(
    groups, members, factor_ref, support_ref, plan_ref, out_ref,
    held, cur, send, recv, raw_out, raw_in, turn_out, turn, acc, gram, gram_in, rot, stack,
    load_sem, move_send, move_recv, raw_send, raw_recv, turn_send, turn_recv, swap_send, swap_recv, sum_send, sum_recv, rot_send, rot_recv,
):
    slots, rows, _ = cur.shape
    size = 2 * W
    chunk = rows // CHUNKS
    chips = members // 2
    stages = chips.bit_length() - 1
    g = lax.axis_index("col")
    m = lax.axis_index("row")
    core = lax.rem(m, 2)
    chip = m // 2
    partner = m + 1 - 2 * core
    half = g // 2
    at_end = jnp.logical_or(g == 0, g == groups - 1)
    inside = jnp.logical_not(at_end)
    goals = [2 - half, g + 1 - 2 * lax.rem(g, 2), 3 - 3 * half]

    def flipped(bit):
        step = 1 << bit
        on = lax.rem(chip // step, 2)
        return (chip + step - 2 * step * on) * 2 + core

    loads = []
    for q in range(CHUNKS):
        span = pl.ds(q * chunk, chunk)
        loads.append(pltpu.make_async_copy(factor_ref.at[span], held.at[span], load_sem.at[q]))
        loads[q].start()

    goal_peers = [{"col": goal, "row": m} for goal in goals]
    row_peers = [{"col": g, "row": partner}]
    row_peers += [{"col": g, "row": flipped(b)} for b in range(stages)]
    barrier = pltpu.get_barrier_semaphore()
    for peer in goal_peers + row_peers:
        pl.semaphore_signal(barrier, inc=1, device_id=peer, device_id_type=MESH)

    row_ids = lax.broadcasted_iota(jnp.int32, (size, size), 0)
    col_ids = lax.broadcasted_iota(jnp.int32, (size, size), 1)
    eye = (row_ids == col_ids).astype(F32)

    def mask(q):
        loads[q].wait()
        for s in range(slots):
            for b in range(q * chunk // RB, (q + 1) * chunk // RB):
                span = pl.ds(b * RB, RB)
                weight = support_ref[b, g * slots + s].astype(F32)
                cur[s, span] = held[span, s * W:(s + 1) * W] * weight

    def before(r, position):
        return position if r == 0 else plan_ref[r - 1, position]

    blocks = groups * slots
    pick, keep, take = [], [], []
    for r in range(ROUNDS):
        dest = []
        for s in range(slots):
            block = before(r, g * slots + s)
            dest.append(sum(
                jnp.where(plan_ref[r, j] == block, j // slots, 0) for j in range(blocks)))

        def slot_for(goal):
            return jnp.minimum(slots - 1, sum(
                jnp.where(dest[s] == goal, s, 0) for s in range(slots)))

        pick.append([slot_for(goal) for goal in goals])
        keep.append(slot_for(g))
        take.append([])
        for s in range(slots):
            block = plan_ref[r, g * slots + s]
            take[r].append(jnp.minimum(groups - 1, sum(
                jnp.where(before(r, j) == block, j // slots, 0) for j in range(blocks))))

    copies = []

    def start(copy):
        copy.start()
        copies.append(copy)
        return copy

    def move(r, q, j, source):
        span = pl.ds(q * chunk, chunk)
        return pltpu.make_async_remote_copy(
            src_ref=send.at[r, j, span],
            dst_ref=recv[r][q].at[source],
            send_sem=move_send.at[r, q, j],
            recv_sem=move_recv.at[r, q, source],
            device_id=goal_peers[j],
            device_id_type=MESH,
        )

    def prepare(r, q):
        span = pl.ds(q * chunk, chunk)
        for j in range(groups - 1):
            send[r, j, span] = cur[pick[r][j], span]
        recv[r][q][g] = cur[keep[r], span]

    def arrive(r, q):
        for s in range(2):
            move(r, q, 0, 2 - 2 * half + s).wait_recv()
        if r == 0:
            move(r, q, 0, goals[1]).wait_recv()
        else:
            @pl.when(at_end)
            def _():
                move(r, q, 0, goals[1]).wait_recv()

    raws = [pltpu.make_async_remote_copy(
        src_ref=raw_out.at[q],
        dst_ref=raw_in.at[q],
        send_sem=raw_send.at[q],
        recv_sem=raw_recv.at[q],
        device_id=goal_peers[1],
        device_id_type=MESH,
    ) for q in range(CHUNKS)]
    near_slot = pick[1][1]
    share = pl.ds(pl.multiple_of(core * W, W), W)
    turn_copy = pltpu.make_async_remote_copy(
        src_ref=turn_out,
        dst_ref=turn.at[share],
        send_sem=turn_send.at[0],
        recv_sem=turn_recv.at[0],
        device_id=goal_peers[1],
        device_id_type=MESH,
    )
    turn_swap = pltpu.make_async_remote_copy(
        src_ref=turn.at[share],
        dst_ref=turn.at[share],
        send_sem=turn_send.at[1],
        recv_sem=turn_recv.at[1],
        device_id=row_peers[0],
        device_id_type=MESH,
    )

    def start_raw(q):
        @pl.when(at_end)
        def _():
            raw_out[q] = load_pair(0, near_slot // 2, q)
            raws[q].start()

    def start_turn():
        @pl.when(at_end)
        def _():
            side = jnp.where(near_slot // 2 == core, 0, 1)
            wide = rot[0, side, share]
            turn_out[...] = jnp.where(lax.rem(near_slot, 2) == 0, wide[:, :W], wide[:, W:])
            turn_copy.start()

    def turn_raws():
        @pl.when(inside)
        def _():
            turn_copy.wait_recv()
            turn_swap.start()
            turn_swap.wait_recv()
            for q in range(CHUNKS):
                raws[q].wait_recv()
                recv[1][q][goals[1]] = dot3(raw_in[q], turn[...])

    def start_near(q):
        @pl.when(inside)
        def _():
            move(1, q, 1, g).start()

    def load_pair(r, k, q):
        first = jnp.where(k == 0, take[r][0], take[r][2])
        last = jnp.where(k == 0, take[r][1], take[r][3])
        return jnp.concatenate([recv[r][q][first], recv[r][q][last]], axis=1)

    mask(0)
    prepare(0, 0)
    pl.semaphore_wait(barrier, groups - 1 + len(row_peers))
    for q in range(CHUNKS):
        if q:
            mask(q)
            prepare(0, q)
        for j in range(groups - 2):
            start(move(0, q, j, g))
    for q in range(CHUNKS):
        start(move(0, q, groups - 2, g))
    for r in range(ROUNDS):
        if r == 1:
            turn_raws()
        for q in range(CHUNKS):
            arrive(r, q)
            if r == 0:
                start_raw(q)
            for k in range(2):
                high, low = split(load_pair(r, k, q))
                mixed = dot_t(high, low)
                part = dot_t(high, high) + (mixed + mixed.T)
                acc[k] = part if q == 0 else acc[k] + part
        for k in range(2):
            cross, tile, diagonal = pack(acc[k])
            gram_in[r, k, :W] = cross
            gram_in[r, k, W:size] = tile
            gram_in[r, k, size:] = diagonal
        swap = start(pltpu.make_async_remote_copy(
            src_ref=gram_in.at[r, 1 - core],
            dst_ref=gram_in.at[r, 2],
            send_sem=swap_send.at[r],
            recv_sem=swap_recv.at[r],
            device_id=row_peers[0],
            device_id_type=MESH,
        ))
        swap.wait_recv()
        total = gram_in[r, core] + gram_in[r, 2]
        for stage in range(stages):
            gram[r, 2 * stage] = total
            pair = []
            for h in range(2):
                bit = (stage + h * (stages // 2)) % stages
                part = pl.ds(0, W) if h == 0 else pl.ds(W, W + 8)
                pair.append(start(pltpu.make_async_remote_copy(
                    src_ref=gram.at[r, 2 * stage, part],
                    dst_ref=gram.at[r, 2 * stage + 1, part],
                    send_sem=sum_send.at[r, stage, h],
                    recv_sem=sum_recv.at[r, stage, h],
                    device_id=row_peers[1 + bit],
                    device_id_type=MESH,
                )))
            for copy in pair:
                copy.wait_recv()
            total = total + gram[r, 2 * stage + 1]
        rot[r, 0] = rotation(unpack(total), eye, stack)
        back = start(pltpu.make_async_remote_copy(
            src_ref=rot.at[r, 0],
            dst_ref=rot.at[r, 1],
            send_sem=rot_send.at[r],
            recv_sem=rot_recv.at[r],
            device_id=row_peers[0],
            device_id_type=MESH,
        ))
        for side in range(2):
            k = core if side == 0 else 1 - core
            if side == 1:
                back.wait_recv()
            if side == 1 and r == 0:
                start_turn()
            for q in range(CHUNKS):
                span = pl.ds(q * chunk, chunk)
                turned = dot3(load_pair(r, k, q), rot[r, side])
                if r == ROUNDS - 1:
                    lanes = pl.ds(pl.multiple_of(k * size, size), size)
                    out_ref[span, lanes] = turned
                else:
                    cur[2 * k, span] = turned[:, :W]
                    cur[2 * k + 1, span] = turned[:, W:]
                    if side == 1:
                        prepare(r + 1, q)
                        for j in (0, groups - 2):
                            start(move(r + 1, q, j, g))
                        start_near(q)
    @pl.when(at_end)
    def _():
        for copy in [*raws, turn_copy]:
            copy.wait_send()

    @pl.when(inside)
    def _():
        turn_swap.wait_send()
        for q in range(CHUNKS):
            move(1, q, 1, g).wait_send()

    for copy in copies:
        copy.wait_send()


def on_device(groups, members, factor, support, plan):
    rows = factor.shape[0]
    slots = factor.shape[1] // W
    chips = members // 2
    stages = chips.bit_length() - 1
    assert slots == 4 and groups == 4 and chips == 1 << stages and stages >= 1 and ROUNDS == 2
    size = 2 * W
    dma = pltpu.SemaphoreType.DMA
    smem = pl.BlockSpec(memory_space=pltpu.SMEM)
    return pl.pallas_call(
        functools.partial(kernel, groups, members),
        out_shape=jax.ShapeDtypeStruct(factor.shape, F32),
        in_specs=[pl.BlockSpec(memory_space=pl.ANY), smem, smem],
        out_specs=pl.BlockSpec(memory_space=pltpu.VMEM),
        scratch_shapes=[
            pltpu.VMEM(factor.shape, F32),
            pltpu.VMEM((slots, rows, W), F32),
            pltpu.VMEM((ROUNDS, groups - 1, rows, W), F32),
            [[pltpu.VMEM((groups, rows // CHUNKS, W), F32)] * CHUNKS] * ROUNDS,
            pltpu.VMEM((CHUNKS, rows // CHUNKS, size), F32),
            pltpu.VMEM((CHUNKS, rows // CHUNKS, size), F32),
            pltpu.VMEM((W, W), F32),
            pltpu.VMEM((size, W), F32),
            pltpu.VMEM((2, size, size), F32),
            pltpu.VMEM((ROUNDS, 2 * stages, size + 8, W), F32),
            pltpu.VMEM((ROUNDS, 3, size + 8, W), F32),
            pltpu.VMEM((ROUNDS, 2, size, size), F32),
            pltpu.VMEM((2 * size, size), F32),
            dma((CHUNKS,)),
            dma((ROUNDS, CHUNKS, groups - 1)),
            dma((ROUNDS, CHUNKS, groups)),
            dma((CHUNKS,)),
            dma((CHUNKS,)),
            dma((2,)),
            dma((2,)),
            dma((ROUNDS,)),
            dma((ROUNDS,)),
            dma((ROUNDS, stages, 2)),
            dma((ROUNDS, stages, 2)),
            dma((ROUNDS,)),
            dma((ROUNDS,)),
        ],
        compiler_params=pltpu.CompilerParams(
            collective_id=0, has_side_effects=True, vmem_limit_bytes=30 * 1024 * 1024
        ),
    )(*(pltpu.with_memory_space_constraint(x, pltpu.HBM) for x in (factor, support.T, plan)))


def solution(mesh):
    return jax.shard_map(
        functools.partial(on_device, mesh.shape["col"], mesh.shape["row"]),
        mesh=mesh,
        in_specs=(P("row", "col"), P(None, "row"), P()),
        out_specs=P("row", "col"),
        check_vma=False,
    )
```

```python
import functools

import jax
import jax.numpy as jnp
from jax import lax
from jax.experimental import pallas as pl
from jax.experimental.pallas import tpu as pltpu
from jax.sharding import PartitionSpec as P

W = 128
RB = 128
ROUNDS = 2
CHUNKS = 4
STEPS = 7
DAMPING = 0.01
RELAY = 128
TOP = 2020.0
F32 = jnp.float32
BF16 = jnp.bfloat16
MESH = pl.DeviceIdType.MESH


def split(x):
    high = x.astype(BF16)
    return high, (x - high.astype(F32)).astype(BF16)


def dot(a, b):
    return jnp.dot(a, b, preferred_element_type=F32)


def dot3(a, b):
    a_high, a_low = split(a)
    b_high, b_low = split(b)
    return dot(a_high, b_high) + (dot(a_high, b_low) + dot(a_low, b_high))


def dot_t(a, b):
    return lax.dot_general(a, b, (((0,), (0,)), ((), ())), preferred_element_type=F32)


def rotation(gram, eye, stack):
    size = gram.shape[0]
    on_diagonal = gram * eye
    diag_rows = jnp.sum(on_diagonal, axis=1, keepdims=True)
    diag_cols = jnp.sum(on_diagonal, axis=0, keepdims=True)
    spread = diag_rows - diag_cols
    joined = diag_rows + diag_cols
    half = 0.5 * gram * spread / (spread * spread + gram * gram + DAMPING * joined * joined)
    squared = dot3(half, half)
    stack[:size] = eye - squared
    stack[size:] = eye - half
    scales, low, high = [], 1.0, TOP
    for _ in range(STEPS):
        scales.append(2.0 / (low + high))
        low, high = 4.0 * low * high / (low + high) ** 2, 1.0

    def factor(scale):
        return (2.0 * scale) * eye - (scale * scale) * stack[:size]

    def scaled(step, carry):
        scale = jnp.float32(scales[0])
        for i in range(1, STEPS - 1):
            scale = jnp.where(step == i, scales[i], scale)
        stack[...] = dot3(stack[...], factor(scale))
        return carry

    lax.fori_loop(0, STEPS - 1, scaled, 0)
    inverse = dot3(stack[size:], factor(scales[-1]))
    residual = (eye - inverse) - dot3(half, inverse)
    short = residual.astype(BF16)
    inverse = inverse + dot3(inverse, residual + dot(short, short))
    return 2.0 * inverse - eye


def pack(gram):
    first, last = gram[:W, :W], gram[W:, W:]
    row_ids = lax.broadcasted_iota(jnp.int32, (W, W), 0)
    col_ids = lax.broadcasted_iota(jnp.int32, (W, W), 1)
    tile = jnp.where(row_ids >= col_ids, first, last)
    diagonal = jnp.sum(jnp.where(row_ids == col_ids, last, 0.0), axis=0, keepdims=True)
    return gram[:W, W:], tile, jnp.broadcast_to(diagonal, (8, W))


def unpack(cross, tile, diagonal):
    row_ids = lax.broadcasted_iota(jnp.int32, (W, W), 0)
    col_ids = lax.broadcasted_iota(jnp.int32, (W, W), 1)
    lower = jnp.where(row_ids > col_ids, tile, 0.0)
    upper = jnp.where(row_ids < col_ids, tile, 0.0)
    first = lower + lower.T + jnp.where(row_ids == col_ids, tile, 0.0)
    last = upper + upper.T + jnp.where(row_ids == col_ids, diagonal, 0.0)
    top = jnp.concatenate([first, cross], axis=1)
    return jnp.concatenate([top, jnp.concatenate([cross.T, last], axis=1)], axis=0)


def kernel(
    groups, members, factor_ref, support_ref, plan_ref, out_ref,
    held, cur, send, recv, late, relay, raw_out, raw_in, turn_out, turn, acc, gram, gram_in,
    piece, piece_in, whole, rot, stack,
    go_sem, relay_send, relay_recv, pass_send, pass_recv, load_sem, move_send, move_recv, raw_send, raw_recv, turn_send, turn_recv, swap_send, swap_recv, sum_send, sum_recv, rot_send, rot_recv, whole_send, whole_recv,
):
    slots, rows, _ = cur.shape
    size = 2 * W
    chunk = rows // CHUNKS
    chips = members // 2
    stages = chips.bit_length() - 1
    g = lax.axis_index("col")
    m = lax.axis_index("row")
    core = lax.rem(m, 2)
    chip = m // 2
    partner = m + 1 - 2 * core
    half = g // 2
    at_end = jnp.logical_or(g == 0, g == groups - 1)
    inside = jnp.logical_not(at_end)
    goals = [2 - half, g + 1 - 2 * lax.rem(g, 2), 3 - 3 * half]

    def flipped(bit):
        step = 1 << bit
        on = lax.rem(chip // step, 2)
        return (chip + step - 2 * step * on) * 2 + core

    loads = []
    for q in range(CHUNKS):
        span = pl.ds(q * chunk, chunk)
        loads.append(pltpu.make_async_copy(factor_ref.at[span], held.at[span], load_sem.at[q]))
        loads[q].start()

    goal_peers = [{"col": goal, "row": m} for goal in goals]
    row_peers = [{"col": g, "row": partner}]
    row_peers += [{"col": g, "row": flipped(b)} for b in range(stages)]
    barrier = pltpu.get_barrier_semaphore()
    for peer in goal_peers + row_peers:
        pl.semaphore_signal(barrier, inc=1, device_id=peer, device_id_type=MESH)

    row_ids = lax.broadcasted_iota(jnp.int32, (size, size), 0)
    col_ids = lax.broadcasted_iota(jnp.int32, (size, size), 1)
    eye = (row_ids == col_ids).astype(F32)

    def mask(q):
        loads[q].wait()
        for s in range(slots):
            for b in range(q * chunk // RB, (q + 1) * chunk // RB):
                span = pl.ds(b * RB, RB)
                weight = support_ref[b, g * slots + s].astype(F32)
                cur[s, span] = held[span, s * W:(s + 1) * W] * weight

    def before(r, position):
        return position if r == 0 else plan_ref[r - 1, position]

    blocks = groups * slots
    pick, keep, take = [], [], []
    for r in range(ROUNDS):
        dest = []
        for s in range(slots):
            block = before(r, g * slots + s)
            dest.append(sum(
                jnp.where(plan_ref[r, j] == block, j // slots, 0) for j in range(blocks)))

        def slot_for(goal):
            return jnp.minimum(slots - 1, sum(
                jnp.where(dest[s] == goal, s, 0) for s in range(slots)))

        pick.append([slot_for(goal) for goal in goals])
        keep.append(slot_for(g))
        take.append([])
        for s in range(slots):
            block = plan_ref[r, g * slots + s]
            take[r].append(jnp.minimum(groups - 1, sum(
                jnp.where(before(r, j) == block, j // slots, 0) for j in range(blocks))))

    copies = []

    def start(copy):
        copy.start()
        copies.append(copy)
        return copy

    def move(r, q, j, source, last=False):
        count = chunk - RELAY if last and q == CHUNKS - 1 else chunk
        landing = late[q] if last else recv[r][q].at[source]
        return pltpu.make_async_remote_copy(
            src_ref=send.at[r, j, pl.ds(q * chunk, count)],
            dst_ref=landing.at[pl.ds(0, count)],
            send_sem=move_send.at[r, q, j],
            recv_sem=move_recv.at[r, q, source],
            device_id=goal_peers[j],
            device_id_type=MESH,
        )

    across = (0, groups - 2)
    relays = [pltpu.make_async_remote_copy(
        src_ref=send.at[1, j, pl.ds(rows - RELAY, RELAY)],
        dst_ref=relay.at[i],
        send_sem=relay_send.at[i],
        recv_sem=relay_recv.at[i],
        device_id=goal_peers[1],
        device_id_type=MESH,
    ) for i, j in enumerate(across)]
    passes = [pltpu.make_async_remote_copy(
        src_ref=relay.at[i],
        dst_ref=late[CHUNKS - 1].at[pl.ds(chunk - RELAY, RELAY)],
        send_sem=pass_send.at[i],
        recv_sem=pass_recv.at[0],
        device_id=goal_peers[j],
        device_id_type=MESH,
    ) for i, j in enumerate(across)]

    def prepare(r, q):
        span = pl.ds(q * chunk, chunk)
        for j in range(groups - 1):
            send[r, j, span] = cur[pick[r][j], span]
        recv[r][q][g] = cur[keep[r], span]

    def arrive_first(q):
        for source in goals:
            move(0, q, 0, source).wait_recv()

    def arrive_early(q):
        move(1, q, 0, goals[0]).wait_recv()

        @pl.when(at_end)
        def _():
            move(1, q, 0, goals[1]).wait_recv()

    def arrive_late(q):
        move(1, q, 0, goals[2], True).wait_recv()
        if q == CHUNKS - 1:
            passes[0].wait_recv()

    raws = [pltpu.make_async_remote_copy(
        src_ref=raw_out.at[q],
        dst_ref=raw_in.at[q],
        send_sem=raw_send.at[q],
        recv_sem=raw_recv.at[q],
        device_id=goal_peers[1],
        device_id_type=MESH,
    ) for q in range(CHUNKS)]
    near_slot = pick[1][1]
    share = pl.ds(pl.multiple_of(core * W, W), W)
    turn_copy = pltpu.make_async_remote_copy(
        src_ref=turn_out,
        dst_ref=turn.at[share],
        send_sem=turn_send.at[0],
        recv_sem=turn_recv.at[0],
        device_id=goal_peers[1],
        device_id_type=MESH,
    )
    turn_swap = pltpu.make_async_remote_copy(
        src_ref=turn.at[share],
        dst_ref=turn.at[share],
        send_sem=turn_send.at[1],
        recv_sem=turn_recv.at[1],
        device_id=row_peers[0],
        device_id_type=MESH,
    )

    def start_raw(q):
        @pl.when(at_end)
        def _():
            raw_out[q] = load_pair(near_slot // 2, q)
            raws[q].start()

    def start_turn():
        @pl.when(at_end)
        def _():
            side = jnp.where(near_slot // 2 == core, 0, 1)
            wide = rot[side, share]
            turn_out[...] = jnp.where(lax.rem(near_slot, 2) == 0, wide[:, :W], wide[:, W:])
            turn_copy.start()

    def turn_raws():
        @pl.when(inside)
        def _():
            turn_copy.wait_recv()
            turn_swap.start()
            turn_swap.wait_recv()
            for q in range(CHUNKS):
                raws[q].wait_recv()
                recv[1][q][goals[1]] = dot3(raw_in[q], turn[...])

    def start_second(q):
        @pl.when(inside)
        def _():
            for j in range(groups - 1):
                move(1, q, j, g).start()

        if q == CHUNKS - 1:
            @pl.when(at_end)
            def _():
                for copy in relays:
                    copy.start()

    def start_far():
        @pl.when(inside)
        def _():
            for q in range(CHUNKS):
                for j in across:
                    move(1, q, j, g).wait_send()
            pl.semaphore_signal(go_sem.at[1], inc=1, device_id=goal_peers[1], device_id_type=MESH)
            for i in range(2):
                relays[i].wait_recv()
                passes[i].start()

        @pl.when(at_end)
        def _():
            pl.semaphore_wait(go_sem.at[1], 1)
            for q in range(CHUNKS):
                for j in across:
                    move(1, q, j, g, True).start()

    def load_pair(k, q):
        first = jnp.where(k == 0, take[0][0], take[0][2])
        last = jnp.where(k == 0, take[0][1], take[0][3])
        return jnp.concatenate([recv[0][q][first], recv[0][q][last]], axis=1)

    far = goals[2]
    late_last = jnp.logical_or(take[1][2] == far, take[1][3] == far)
    late_pair = [jnp.where(late_last, take[1][2 + i], take[1][i]) for i in range(2)]
    early_pair = [jnp.where(late_last, take[1][i], take[1][2 + i]) for i in range(2)]
    far_left = late_pair[0] == far
    late_other = jnp.where(far_left, late_pair[1], late_pair[0])

    def load_early(q):
        return jnp.concatenate([recv[1][q][block] for block in early_pair], axis=1)

    def load_late(q):
        newest, other = late[q][...], recv[1][q][late_other]
        left, right = jnp.where(far_left, newest, other), jnp.where(far_left, other, newest)
        return jnp.concatenate([left, right], axis=1)

    def add_gram(k, q, pair):
        high, low = split(pair)
        mixed = dot_t(high, low)
        part = dot_t(high, high) + (mixed + mixed.T)
        acc[k] = part if q == 0 else acc[k] + part

    def sum_chips(phase, total, slots_ref, cut):
        for stage in range(stages):
            slots_ref[2 * stage] = total
            both = []
            for h in range(2):
                bit = (stage + h * (stages // 2)) % stages
                part = pl.ds(0, cut) if h == 0 else pl.ds(cut, total.shape[0] - cut)
                both.append(start(pltpu.make_async_remote_copy(
                    src_ref=slots_ref.at[2 * stage, part],
                    dst_ref=slots_ref.at[2 * stage + 1, part],
                    send_sem=sum_send.at[phase, stage, h],
                    recv_sem=sum_recv.at[phase, stage, h],
                    device_id=row_peers[1 + bit],
                    device_id_type=MESH,
                )))
            for copy in both:
                copy.wait_recv()
            total = total + slots_ref[2 * stage + 1]
        return total

    def rotation_of(e):
        cross, tile, diagonal = pack(acc[e])
        piece_in[e, 0, :W] = cross
        piece_in[e, 0, W:] = diagonal
        piece_in[e, 1, :W] = tile
        piece_in[e, 1, W:] = diagonal
        start(pltpu.make_async_remote_copy(
            src_ref=piece_in.at[e, 1 - core],
            dst_ref=piece_in.at[e, 2],
            send_sem=swap_send.at[1 + e],
            recv_sem=swap_recv.at[1 + e],
            device_id=row_peers[0],
            device_id_type=MESH,
        )).wait_recv()
        total = sum_chips(1 + e, piece_in[e, core] + piece_in[e, 2], piece.at[e], W // 2)
        whole[e, core] = total
        start(pltpu.make_async_remote_copy(
            src_ref=whole.at[e, core],
            dst_ref=whole.at[e, core],
            send_sem=whole_send.at[e],
            recv_sem=whole_recv.at[e],
            device_id=row_peers[0],
            device_id_type=MESH,
        )).wait_recv()
        return rotation(unpack(whole[e, 0, :W], whole[e, 1, :W], whole[e, 0, W:W + 1]), eye, stack)

    mask(0)
    prepare(0, 0)
    pl.semaphore_wait(barrier, groups - 1 + len(row_peers))
    for q in range(CHUNKS):
        if q:
            mask(q)
            prepare(0, q)
        for j in range(groups - 2):
            start(move(0, q, j, g))
    @pl.when(at_end)
    def _():
        pl.semaphore_wait(go_sem.at[0], 1)
        for q in range(CHUNKS):
            move(0, q, groups - 2, g).start()

    for q in range(CHUNKS):
        arrive_first(q)
        if q == CHUNKS - 2:
            @pl.when(inside)
            def _():
                for c in range(CHUNKS):
                    move(0, c, groups - 2, g).start()
        if q == CHUNKS - 1:
            @pl.when(inside)
            def _():
                pl.semaphore_signal(go_sem.at[0], inc=1, device_id=goal_peers[1], device_id_type=MESH)
        start_raw(q)
        for k in range(2):
            add_gram(k, q, load_pair(k, q))
    for k in range(2):
        cross, tile, diagonal = pack(acc[k])
        gram_in[k, :W] = cross
        gram_in[k, W:size] = tile
        gram_in[k, size:] = diagonal
    start(pltpu.make_async_remote_copy(
        src_ref=gram_in.at[1 - core],
        dst_ref=gram_in.at[2],
        send_sem=swap_send.at[0],
        recv_sem=swap_recv.at[0],
        device_id=row_peers[0],
        device_id_type=MESH,
    )).wait_recv()
    total = sum_chips(0, gram_in[core] + gram_in[2], gram, W)
    rot[0] = rotation(unpack(total[:W], total[W:size], total[size:size + 1]), eye, stack)
    back = start(pltpu.make_async_remote_copy(
        src_ref=rot.at[0],
        dst_ref=rot.at[1],
        send_sem=rot_send.at[0],
        recv_sem=rot_recv.at[0],
        device_id=row_peers[0],
        device_id_type=MESH,
    ))
    for side in range(2):
        k = core if side == 0 else 1 - core
        if side == 1:
            back.wait_recv()
            start_turn()
        for q in (CHUNKS - 1, *range(CHUNKS - 1)):
            span = pl.ds(q * chunk, chunk)
            turned = dot3(load_pair(k, q), rot[side])
            cur[2 * k, span] = turned[:, :W]
            cur[2 * k + 1, span] = turned[:, W:]
            if side == 1:
                prepare(1, q)
                start_second(q)

    start_far()
    turn_raws()
    for q in range(CHUNKS):
        arrive_early(q)
        add_gram(0, q, load_early(q))
    early = rotation_of(0)
    for q in range(CHUNKS):
        held[pl.ds(q * chunk, chunk), :size] = dot3(load_early(q), early)
    for q in range(CHUNKS):
        arrive_late(q)
        add_gram(1, q, load_late(q))
    last = rotation_of(1)
    for q in range(CHUNKS):
        span = pl.ds(q * chunk, chunk)
        turned, ready = dot3(load_late(q), last), held[span, :size]
        out_ref[span, :size] = jnp.where(late_last, ready, turned)
        out_ref[span, size:] = jnp.where(late_last, turned, ready)
    @pl.when(at_end)
    def _():
        for copy in [*raws, turn_copy]:
            copy.wait_send()

    @pl.when(inside)
    def _():
        turn_swap.wait_send()
        for copy in passes:
            copy.wait_send()
        for q in range(CHUNKS):
            move(1, q, 1, g).wait_send()

    for q in range(CHUNKS):
        move(0, q, groups - 2, g).wait_send()

    @pl.when(at_end)
    def _():
        for q in range(CHUNKS):
            for j in across:
                move(1, q, j, g, True).wait_send()
        for copy in relays:
            copy.wait_send()

    for copy in copies:
        copy.wait_send()


def on_device(groups, members, factor, support, plan):
    rows = factor.shape[0]
    slots = factor.shape[1] // W
    chips = members // 2
    stages = chips.bit_length() - 1
    assert slots == 4 and groups == 4 and chips == 1 << stages and stages >= 1 and ROUNDS == 2
    size = 2 * W
    dma = pltpu.SemaphoreType.DMA
    smem = pl.BlockSpec(memory_space=pltpu.SMEM)
    return pl.pallas_call(
        functools.partial(kernel, groups, members),
        out_shape=jax.ShapeDtypeStruct(factor.shape, F32),
        in_specs=[pl.BlockSpec(memory_space=pl.ANY), smem, smem],
        out_specs=pl.BlockSpec(memory_space=pltpu.VMEM),
        scratch_shapes=[
            pltpu.VMEM(factor.shape, F32),
            pltpu.VMEM((slots, rows, W), F32),
            pltpu.VMEM((ROUNDS, groups - 1, rows, W), F32),
            [[pltpu.VMEM((groups, rows // CHUNKS, W), F32)] * CHUNKS] * ROUNDS,
            [pltpu.VMEM((rows // CHUNKS, W), F32)] * CHUNKS,
            pltpu.VMEM((2, RELAY, W), F32),
            pltpu.VMEM((CHUNKS, rows // CHUNKS, size), F32),
            pltpu.VMEM((CHUNKS, rows // CHUNKS, size), F32),
            pltpu.VMEM((W, W), F32),
            pltpu.VMEM((size, W), F32),
            pltpu.VMEM((2, size, size), F32),
            pltpu.VMEM((2 * stages, size + 8, W), F32),
            pltpu.VMEM((3, size + 8, W), F32),
            pltpu.VMEM((2, 2 * stages, W + 8, W), F32),
            pltpu.VMEM((2, 3, W + 8, W), F32),
            pltpu.VMEM((2, 2, W + 8, W), F32),
            pltpu.VMEM((2, size, size), F32),
            pltpu.VMEM((2 * size, size), F32),
            pltpu.SemaphoreType.REGULAR((2,)),
            dma((2,)),
            dma((2,)),
            dma((2,)),
            dma((1,)),
            dma((CHUNKS,)),
            dma((ROUNDS, CHUNKS, groups - 1)),
            dma((ROUNDS, CHUNKS, groups)),
            dma((CHUNKS,)),
            dma((CHUNKS,)),
            dma((2,)),
            dma((2,)),
            dma((3,)),
            dma((3,)),
            dma((3, stages, 2)),
            dma((3, stages, 2)),
            dma((1,)),
            dma((1,)),
            dma((2,)),
            dma((2,)),
        ],
        compiler_params=pltpu.CompilerParams(
            collective_id=0, has_side_effects=True, vmem_limit_bytes=30 * 1024 * 1024
        ),
    )(*(pltpu.with_memory_space_constraint(x, pltpu.HBM) for x in (factor, support.T, plan)))


def solution(mesh):
    return jax.shard_map(
        functools.partial(on_device, mesh.shape["col"], mesh.shape["row"]),
        mesh=mesh,
        in_specs=(P("row", "col"), P(None, "row"), P()),
        out_specs=P("row", "col"),
        check_vma=False,
    )
```

```python
import functools

import jax
import jax.numpy as jnp
from jax import lax
from jax.experimental import pallas as pl
from jax.experimental.pallas import tpu as pltpu
from jax.sharding import PartitionSpec as P

W = 128
RB = 128
ROUNDS = 2
CHUNKS = 4
STEPS = 7
DAMPING = 0.01
RELAY = 128
TOP = 2020.0
F32 = jnp.float32
BF16 = jnp.bfloat16
MESH = pl.DeviceIdType.MESH


def split(x):
    high = x.astype(BF16)
    return high, (x - high.astype(F32)).astype(BF16)


def dot(a, b):
    return jnp.dot(a, b, preferred_element_type=F32)


def dot3(a, b):
    a_high, a_low = split(a)
    b_high, b_low = split(b)
    return dot(a_high, b_high) + (dot(a_high, b_low) + dot(a_low, b_high))


def dot_t(a, b):
    return lax.dot_general(a, b, (((0,), (0,)), ((), ())), preferred_element_type=F32)


def rotation(gram, eye, stack):
    size = gram.shape[0]
    on_diagonal = gram * eye
    diag_rows = jnp.sum(on_diagonal, axis=1, keepdims=True)
    diag_cols = jnp.sum(on_diagonal, axis=0, keepdims=True)
    spread = diag_rows - diag_cols
    joined = diag_rows + diag_cols
    half = 0.5 * gram * spread / (spread * spread + gram * gram + DAMPING * joined * joined)
    squared = dot3(half, half)
    stack[:size] = eye - squared
    stack[size:] = eye - half
    scales, low, high = [], 1.0, TOP
    for _ in range(STEPS):
        scales.append(2.0 / (low + high))
        low, high = 4.0 * low * high / (low + high) ** 2, 1.0

    def factor(scale):
        return (2.0 * scale) * eye - (scale * scale) * stack[:size]

    def scaled(step, carry):
        scale = jnp.float32(scales[0])
        for i in range(1, STEPS - 1):
            scale = jnp.where(step == i, scales[i], scale)
        stack[...] = dot3(stack[...], factor(scale))
        return carry

    lax.fori_loop(0, STEPS - 1, scaled, 0)
    inverse = dot3(stack[size:], factor(scales[-1]))
    residual = (eye - inverse) - dot3(half, inverse)
    short = residual.astype(BF16)
    inverse = inverse + dot3(inverse, residual + dot(short, short))
    return 2.0 * inverse - eye


def pack(gram):
    first, last = gram[:W, :W], gram[W:, W:]
    row_ids = lax.broadcasted_iota(jnp.int32, (W, W), 0)
    col_ids = lax.broadcasted_iota(jnp.int32, (W, W), 1)
    tile = jnp.where(row_ids >= col_ids, first, last)
    diagonal = jnp.sum(jnp.where(row_ids == col_ids, last, 0.0), axis=0, keepdims=True)
    return gram[:W, W:], tile, jnp.broadcast_to(diagonal, (8, W))


def unpack(cross, tile, diagonal):
    row_ids = lax.broadcasted_iota(jnp.int32, (W, W), 0)
    col_ids = lax.broadcasted_iota(jnp.int32, (W, W), 1)
    lower = jnp.where(row_ids > col_ids, tile, 0.0)
    upper = jnp.where(row_ids < col_ids, tile, 0.0)
    first = lower + lower.T + jnp.where(row_ids == col_ids, tile, 0.0)
    last = upper + upper.T + jnp.where(row_ids == col_ids, diagonal, 0.0)
    top = jnp.concatenate([first, cross], axis=1)
    return jnp.concatenate([top, jnp.concatenate([cross.T, last], axis=1)], axis=0)


def kernel(
    groups, members, factor_ref, support_ref, plan_ref, out_ref,
    held, cur, send, recv, late, relay, raw_out, raw_in, turn_out, turn, acc, gram, gram_in,
    piece, piece_in, whole, rot, stack,
    go_sem, relay_send, relay_recv, pass_send, pass_recv, load_sem, move_send, move_recv, raw_send, raw_recv, turn_send, turn_recv, swap_send, swap_recv, sum_send, sum_recv, quad_send, quad_recv, rot_send, rot_recv, whole_send, whole_recv,
):
    slots, rows, _ = cur.shape
    size = 2 * W
    chunk = rows // CHUNKS
    chips = members // 2
    stages = chips.bit_length() - 1
    g = lax.axis_index("col")
    m = lax.axis_index("row")
    core = lax.rem(m, 2)
    chip = m // 2
    partner = m + 1 - 2 * core
    half = g // 2
    at_end = jnp.logical_or(g == 0, g == groups - 1)
    inside = jnp.logical_not(at_end)
    goals = [2 - half, g + 1 - 2 * lax.rem(g, 2), 3 - 3 * half]

    def flipped(bit):
        step = 1 << bit
        on = lax.rem(chip // step, 2)
        return (chip + step - 2 * step * on) * 2 + core

    loads = []
    for q in range(CHUNKS):
        span = pl.ds(q * chunk, chunk)
        loads.append(pltpu.make_async_copy(factor_ref.at[span], held.at[span], load_sem.at[q]))
        loads[q].start()

    goal_peers = [{"col": goal, "row": m} for goal in goals]
    row_peers = [{"col": g, "row": partner}]
    row_peers += [{"col": g, "row": flipped(b)} for b in range(stages)]
    quads = stages // 2
    quad_peers = []
    for b in range(quads):
        one, two = flipped(b), flipped(b + quads)
        quad_peers.append([{"col": g, "row": other} for other in (one, two, one + two - m)])
    diagonals = [quad[2] for quad in quad_peers]
    barrier = pltpu.get_barrier_semaphore()
    for peer in goal_peers + row_peers + diagonals:
        pl.semaphore_signal(barrier, inc=1, device_id=peer, device_id_type=MESH)

    row_ids = lax.broadcasted_iota(jnp.int32, (size, size), 0)
    col_ids = lax.broadcasted_iota(jnp.int32, (size, size), 1)
    eye = (row_ids == col_ids).astype(F32)

    def mask(q):
        loads[q].wait()
        for s in range(slots):
            for b in range(q * chunk // RB, (q + 1) * chunk // RB):
                span = pl.ds(b * RB, RB)
                weight = support_ref[b, g * slots + s].astype(F32)
                cur[s, span] = held[span, s * W:(s + 1) * W] * weight

    def before(r, position):
        return position if r == 0 else plan_ref[r - 1, position]

    blocks = groups * slots
    pick, keep, take = [], [], []
    for r in range(ROUNDS):
        dest = []
        for s in range(slots):
            block = before(r, g * slots + s)
            dest.append(sum(
                jnp.where(plan_ref[r, j] == block, j // slots, 0) for j in range(blocks)))

        def slot_for(goal):
            return jnp.minimum(slots - 1, sum(
                jnp.where(dest[s] == goal, s, 0) for s in range(slots)))

        pick.append([slot_for(goal) for goal in goals])
        keep.append(slot_for(g))
        take.append([])
        for s in range(slots):
            block = plan_ref[r, g * slots + s]
            take[r].append(jnp.minimum(groups - 1, sum(
                jnp.where(before(r, j) == block, j // slots, 0) for j in range(blocks))))

    copies = []

    def start(copy):
        copy.start()
        copies.append(copy)
        return copy

    def move(r, q, j, source, last=False):
        count = chunk - RELAY if last and q == CHUNKS - 1 else chunk
        landing = late[q] if last else recv[r][q].at[source]
        return pltpu.make_async_remote_copy(
            src_ref=send.at[r, j, pl.ds(q * chunk, count)],
            dst_ref=landing.at[pl.ds(0, count)],
            send_sem=move_send.at[r, q, j],
            recv_sem=move_recv.at[r, q, source],
            device_id=goal_peers[j],
            device_id_type=MESH,
        )

    across = (0, groups - 2)
    relays = [pltpu.make_async_remote_copy(
        src_ref=send.at[1, j, pl.ds(rows - RELAY, RELAY)],
        dst_ref=relay.at[i],
        send_sem=relay_send.at[i],
        recv_sem=relay_recv.at[i],
        device_id=goal_peers[1],
        device_id_type=MESH,
    ) for i, j in enumerate(across)]
    passes = [pltpu.make_async_remote_copy(
        src_ref=relay.at[i],
        dst_ref=late[CHUNKS - 1].at[pl.ds(chunk - RELAY, RELAY)],
        send_sem=pass_send.at[i],
        recv_sem=pass_recv.at[0],
        device_id=goal_peers[j],
        device_id_type=MESH,
    ) for i, j in enumerate(across)]

    def prepare(r, q):
        span = pl.ds(q * chunk, chunk)
        for j in range(groups - 1):
            send[r, j, span] = cur[pick[r][j], span]
        recv[r][q][g] = cur[keep[r], span]

    def arrive_first(q):
        for source in goals:
            move(0, q, 0, source).wait_recv()

    def arrive_early(q):
        move(1, q, 0, goals[0]).wait_recv()

        @pl.when(at_end)
        def _():
            move(1, q, 0, goals[1]).wait_recv()

    def arrive_late(q):
        move(1, q, 0, goals[2], True).wait_recv()
        if q == CHUNKS - 1:
            passes[0].wait_recv()

    raws = [pltpu.make_async_remote_copy(
        src_ref=raw_out.at[q],
        dst_ref=raw_in.at[q],
        send_sem=raw_send.at[q],
        recv_sem=raw_recv.at[q],
        device_id=goal_peers[1],
        device_id_type=MESH,
    ) for q in range(CHUNKS)]
    near_slot = pick[1][1]
    share = pl.ds(pl.multiple_of(core * W, W), W)
    turn_copy = pltpu.make_async_remote_copy(
        src_ref=turn_out,
        dst_ref=turn.at[share],
        send_sem=turn_send.at[0],
        recv_sem=turn_recv.at[0],
        device_id=goal_peers[1],
        device_id_type=MESH,
    )
    turn_swap = pltpu.make_async_remote_copy(
        src_ref=turn.at[share],
        dst_ref=turn.at[share],
        send_sem=turn_send.at[1],
        recv_sem=turn_recv.at[1],
        device_id=row_peers[0],
        device_id_type=MESH,
    )

    def start_raw(q):
        @pl.when(at_end)
        def _():
            raw_out[q] = load_pair(near_slot // 2, q)
            raws[q].start()

    def start_turn():
        @pl.when(at_end)
        def _():
            side = jnp.where(near_slot // 2 == core, 0, 1)
            wide = rot[side, share]
            turn_out[...] = jnp.where(lax.rem(near_slot, 2) == 0, wide[:, :W], wide[:, W:])
            turn_copy.start()

    def turn_raws():
        @pl.when(inside)
        def _():
            turn_copy.wait_recv()
            turn_swap.start()
            turn_swap.wait_recv()
            for q in range(CHUNKS):
                raws[q].wait_recv()
                recv[1][q][goals[1]] = dot3(raw_in[q], turn[...])

    def start_second(q):
        @pl.when(inside)
        def _():
            for j in range(groups - 1):
                move(1, q, j, g).start()

        if q == CHUNKS - 1:
            @pl.when(at_end)
            def _():
                for copy in relays:
                    copy.start()

    def start_far():
        @pl.when(inside)
        def _():
            for q in range(CHUNKS):
                for j in across:
                    move(1, q, j, g).wait_send()
            pl.semaphore_signal(go_sem.at[1], inc=1, device_id=goal_peers[1], device_id_type=MESH)
            for i in range(2):
                relays[i].wait_recv()
                passes[i].start()

        @pl.when(at_end)
        def _():
            pl.semaphore_wait(go_sem.at[1], 1)
            for q in range(CHUNKS):
                for j in across:
                    move(1, q, j, g, True).start()

    def load_pair(k, q):
        first = jnp.where(k == 0, take[0][0], take[0][2])
        last = jnp.where(k == 0, take[0][1], take[0][3])
        return jnp.concatenate([recv[0][q][first], recv[0][q][last]], axis=1)

    far = goals[2]
    late_last = jnp.logical_or(take[1][2] == far, take[1][3] == far)
    late_pair = [jnp.where(late_last, take[1][2 + i], take[1][i]) for i in range(2)]
    early_pair = [jnp.where(late_last, take[1][i], take[1][2 + i]) for i in range(2)]
    far_left = late_pair[0] == far
    late_other = jnp.where(far_left, late_pair[1], late_pair[0])

    def load_early(q):
        return jnp.concatenate([recv[1][q][block] for block in early_pair], axis=1)

    def load_late(q):
        newest, other = late[q][...], recv[1][q][late_other]
        left, right = jnp.where(far_left, newest, other), jnp.where(far_left, other, newest)
        return jnp.concatenate([left, right], axis=1)

    def add_gram(k, q, pair):
        high, low = split(pair)
        mixed = dot_t(high, low)
        part = dot_t(high, high) + (mixed + mixed.T)
        acc[k] = part if q == 0 else acc[k] + part

    def sum_chips(total, slots_ref, cut):
        for stage in range(stages):
            slots_ref[2 * stage] = total
            both = []
            for h in range(2):
                bit = (stage + h * (stages // 2)) % stages
                part = pl.ds(0, cut) if h == 0 else pl.ds(cut, total.shape[0] - cut)
                both.append(start(pltpu.make_async_remote_copy(
                    src_ref=slots_ref.at[2 * stage, part],
                    dst_ref=slots_ref.at[2 * stage + 1, part],
                    send_sem=sum_send.at[stage, h],
                    recv_sem=sum_recv.at[stage, h],
                    device_id=row_peers[1 + bit],
                    device_id_type=MESH,
                )))
            for copy in both:
                copy.wait_recv()
            total = total + slots_ref[2 * stage + 1]
        return total

    def sum_quads(e, total):
        for step in range(quads):
            piece[e, 4 * step] = total
            three = [start(pltpu.make_async_remote_copy(
                src_ref=piece.at[e, 4 * step],
                dst_ref=piece.at[e, 4 * step + 1 + i],
                send_sem=quad_send.at[e, step, i],
                recv_sem=quad_recv.at[e, step, i],
                device_id=quad_peers[step][i],
                device_id_type=MESH,
            )) for i in (2, 0, 1)]
            for copy in three:
                copy.wait_recv()
            pair, other = (piece[e, 4 * step + 2 * i] + piece[e, 4 * step + 2 * i + 1] for i in range(2))
            total = pair + other
        return total

    def rotation_of(e):
        cross, tile, diagonal = pack(acc[e])
        piece_in[e, 0, :W] = cross
        piece_in[e, 0, W:] = diagonal
        piece_in[e, 1, :W] = tile
        piece_in[e, 1, W:] = diagonal
        start(pltpu.make_async_remote_copy(
            src_ref=piece_in.at[e, 1 - core],
            dst_ref=piece_in.at[e, 2],
            send_sem=swap_send.at[1 + e],
            recv_sem=swap_recv.at[1 + e],
            device_id=row_peers[0],
            device_id_type=MESH,
        )).wait_recv()
        total = sum_quads(e, piece_in[e, core] + piece_in[e, 2])
        whole[e, core] = total
        start(pltpu.make_async_remote_copy(
            src_ref=whole.at[e, core],
            dst_ref=whole.at[e, core],
            send_sem=whole_send.at[e],
            recv_sem=whole_recv.at[e],
            device_id=row_peers[0],
            device_id_type=MESH,
        )).wait_recv()
        return rotation(unpack(whole[e, 0, :W], whole[e, 1, :W], whole[e, 0, W:W + 1]), eye, stack)

    mask(0)
    prepare(0, 0)
    pl.semaphore_wait(barrier, groups - 1 + len(row_peers) + quads)
    for q in range(CHUNKS):
        if q:
            mask(q)
            prepare(0, q)
        for j in range(groups - 2):
            start(move(0, q, j, g))
    @pl.when(at_end)
    def _():
        pl.semaphore_wait(go_sem.at[0], 1)
        for q in range(CHUNKS):
            move(0, q, groups - 2, g).start()

    for q in range(CHUNKS):
        arrive_first(q)
        if q == CHUNKS - 2:
            @pl.when(inside)
            def _():
                for c in range(CHUNKS):
                    move(0, c, groups - 2, g).start()
        if q == CHUNKS - 1:
            @pl.when(inside)
            def _():
                pl.semaphore_signal(go_sem.at[0], inc=1, device_id=goal_peers[1], device_id_type=MESH)
        start_raw(q)
        for k in range(2):
            add_gram(k, q, load_pair(k, q))
    for k in range(2):
        cross, tile, diagonal = pack(acc[k])
        gram_in[k, :W] = cross
        gram_in[k, W:size] = tile
        gram_in[k, size:] = diagonal
    start(pltpu.make_async_remote_copy(
        src_ref=gram_in.at[1 - core],
        dst_ref=gram_in.at[2],
        send_sem=swap_send.at[0],
        recv_sem=swap_recv.at[0],
        device_id=row_peers[0],
        device_id_type=MESH,
    )).wait_recv()
    total = sum_chips(gram_in[core] + gram_in[2], gram, W)
    rot[0] = rotation(unpack(total[:W], total[W:size], total[size:size + 1]), eye, stack)
    back = start(pltpu.make_async_remote_copy(
        src_ref=rot.at[0],
        dst_ref=rot.at[1],
        send_sem=rot_send.at[0],
        recv_sem=rot_recv.at[0],
        device_id=row_peers[0],
        device_id_type=MESH,
    ))
    for side in range(2):
        k = core if side == 0 else 1 - core
        if side == 1:
            back.wait_recv()
            start_turn()
        for q in (CHUNKS - 1, *range(CHUNKS - 1)):
            span = pl.ds(q * chunk, chunk)
            turned = dot3(load_pair(k, q), rot[side])
            cur[2 * k, span] = turned[:, :W]
            cur[2 * k + 1, span] = turned[:, W:]
            if side == 1:
                prepare(1, q)
                start_second(q)

    start_far()
    turn_raws()
    for q in range(CHUNKS):
        arrive_early(q)
        add_gram(0, q, load_early(q))
    early = rotation_of(0)
    for q in range(CHUNKS):
        held[pl.ds(q * chunk, chunk), :size] = dot3(load_early(q), early)
    for q in range(CHUNKS):
        arrive_late(q)
        add_gram(1, q, load_late(q))
    last = rotation_of(1)
    for q in range(CHUNKS):
        span = pl.ds(q * chunk, chunk)
        turned, ready = dot3(load_late(q), last), held[span, :size]
        out_ref[span, :size] = jnp.where(late_last, ready, turned)
        out_ref[span, size:] = jnp.where(late_last, turned, ready)
    @pl.when(at_end)
    def _():
        for copy in [*raws, turn_copy]:
            copy.wait_send()

    @pl.when(inside)
    def _():
        turn_swap.wait_send()
        for copy in passes:
            copy.wait_send()
        for q in range(CHUNKS):
            move(1, q, 1, g).wait_send()

    for q in range(CHUNKS):
        move(0, q, groups - 2, g).wait_send()

    @pl.when(at_end)
    def _():
        for q in range(CHUNKS):
            for j in across:
                move(1, q, j, g, True).wait_send()
        for copy in relays:
            copy.wait_send()

    for copy in copies:
        copy.wait_send()


def on_device(groups, members, factor, support, plan):
    rows = factor.shape[0]
    slots = factor.shape[1] // W
    chips = members // 2
    stages = chips.bit_length() - 1
    assert slots == 4 and groups == 4 and chips == 1 << stages and stages % 2 == 0 and ROUNDS == 2
    size = 2 * W
    dma = pltpu.SemaphoreType.DMA
    smem = pl.BlockSpec(memory_space=pltpu.SMEM)
    return pl.pallas_call(
        functools.partial(kernel, groups, members),
        out_shape=jax.ShapeDtypeStruct(factor.shape, F32),
        in_specs=[pl.BlockSpec(memory_space=pl.ANY), smem, smem],
        out_specs=pl.BlockSpec(memory_space=pltpu.VMEM),
        scratch_shapes=[
            pltpu.VMEM(factor.shape, F32),
            pltpu.VMEM((slots, rows, W), F32),
            pltpu.VMEM((ROUNDS, groups - 1, rows, W), F32),
            [[pltpu.VMEM((groups, rows // CHUNKS, W), F32)] * CHUNKS] * ROUNDS,
            [pltpu.VMEM((rows // CHUNKS, W), F32)] * CHUNKS,
            pltpu.VMEM((2, RELAY, W), F32),
            pltpu.VMEM((CHUNKS, rows // CHUNKS, size), F32),
            pltpu.VMEM((CHUNKS, rows // CHUNKS, size), F32),
            pltpu.VMEM((W, W), F32),
            pltpu.VMEM((size, W), F32),
            pltpu.VMEM((2, size, size), F32),
            pltpu.VMEM((2 * stages, size + 8, W), F32),
            pltpu.VMEM((3, size + 8, W), F32),
            pltpu.VMEM((2, 2 * stages, W + 8, W), F32),
            pltpu.VMEM((2, 3, W + 8, W), F32),
            pltpu.VMEM((2, 2, W + 8, W), F32),
            pltpu.VMEM((2, size, size), F32),
            pltpu.VMEM((2 * size, size), F32),
            pltpu.SemaphoreType.REGULAR((2,)),
            dma((2,)),
            dma((2,)),
            dma((2,)),
            dma((1,)),
            dma((CHUNKS,)),
            dma((ROUNDS, CHUNKS, groups - 1)),
            dma((ROUNDS, CHUNKS, groups)),
            dma((CHUNKS,)),
            dma((CHUNKS,)),
            dma((2,)),
            dma((2,)),
            dma((3,)),
            dma((3,)),
            dma((stages, 2)),
            dma((stages, 2)),
            dma((2, stages // 2, 3)),
            dma((2, stages // 2, 3)),
            dma((1,)),
            dma((1,)),
            dma((2,)),
            dma((2,)),
        ],
        compiler_params=pltpu.CompilerParams(
            collective_id=0, has_side_effects=True, vmem_limit_bytes=30 * 1024 * 1024
        ),
    )(*(pltpu.with_memory_space_constraint(x, pltpu.HBM) for x in (factor, support.T, plan)))


def solution(mesh):
    return jax.shard_map(
        functools.partial(on_device, mesh.shape["col"], mesh.shape["row"]),
        mesh=mesh,
        in_specs=(P("row", "col"), P(None, "row"), P()),
        out_specs=P("row", "col"),
        check_vma=False,
    )
```

```python
import functools

import jax
import jax.numpy as jnp
from jax import lax
from jax.experimental import pallas as pl
from jax.experimental.pallas import tpu as pltpu
from jax.sharding import PartitionSpec as P

W = 128
RB = 128
ROUNDS = 2
CHUNKS = 4
STEPS = 7
DAMPING = 0.01
RELAY = 160
TOP = 2020.0
F32 = jnp.float32
BF16 = jnp.bfloat16
MESH = pl.DeviceIdType.MESH


def split(x):
    high = x.astype(BF16)
    return high, (x - high.astype(F32)).astype(BF16)


def dot(a, b):
    return jnp.dot(a, b, preferred_element_type=F32)


def dot3(a, b):
    a_high, a_low = split(a)
    b_high, b_low = split(b)
    return dot(a_high, b_high) + (dot(a_high, b_low) + dot(a_low, b_high))


def dot_t(a, b):
    return lax.dot_general(a, b, (((0,), (0,)), ((), ())), preferred_element_type=F32)


def rotation(gram, eye, stack):
    size = gram.shape[0]
    on_diagonal = gram * eye
    diag_rows = jnp.sum(on_diagonal, axis=1, keepdims=True)
    diag_cols = jnp.sum(on_diagonal, axis=0, keepdims=True)
    spread = diag_rows - diag_cols
    joined = diag_rows + diag_cols
    half = 0.5 * gram * spread / (spread * spread + gram * gram + DAMPING * joined * joined)
    squared = dot3(half, half)
    stack[:size] = eye - squared
    stack[size:] = eye - half
    scales, low, high = [], 1.0, TOP
    for _ in range(STEPS):
        scales.append(2.0 / (low + high))
        low, high = 4.0 * low * high / (low + high) ** 2, 1.0

    def factor(scale):
        return (2.0 * scale) * eye - (scale * scale) * stack[:size]

    def scaled(step, carry):
        scale = jnp.float32(scales[0])
        for i in range(1, STEPS - 1):
            scale = jnp.where(step == i, scales[i], scale)
        stack[...] = dot3(stack[...], factor(scale))
        return carry

    lax.fori_loop(0, STEPS - 1, scaled, 0)
    inverse = dot3(stack[size:], factor(scales[-1]))
    residual = (eye - inverse) - dot3(half, inverse)
    short = residual.astype(BF16)
    inverse = inverse + dot3(inverse, residual + dot(short, short))
    return 2.0 * inverse - eye


def pack(gram):
    first, last = gram[:W, :W], gram[W:, W:]
    row_ids = lax.broadcasted_iota(jnp.int32, (W, W), 0)
    col_ids = lax.broadcasted_iota(jnp.int32, (W, W), 1)
    tile = jnp.where(row_ids >= col_ids, first, last)
    diagonal = jnp.sum(jnp.where(row_ids == col_ids, last, 0.0), axis=0, keepdims=True)
    return gram[:W, W:], tile, jnp.broadcast_to(diagonal, (8, W))


def unpack(cross, tile, diagonal):
    row_ids = lax.broadcasted_iota(jnp.int32, (W, W), 0)
    col_ids = lax.broadcasted_iota(jnp.int32, (W, W), 1)
    lower = jnp.where(row_ids > col_ids, tile, 0.0)
    upper = jnp.where(row_ids < col_ids, tile, 0.0)
    first = lower + lower.T + jnp.where(row_ids == col_ids, tile, 0.0)
    last = upper + upper.T + jnp.where(row_ids == col_ids, diagonal, 0.0)
    top = jnp.concatenate([first, cross], axis=1)
    return jnp.concatenate([top, jnp.concatenate([cross.T, last], axis=1)], axis=0)


def kernel(
    groups, members, factor_ref, support_ref, plan_ref, out_ref,
    held, cur, send, recv, late, relay, raw_out, raw_in, turn_out, turn, acc, gram, gram_in,
    piece, piece_in, whole, rot, stack,
    go_sem, relay_send, relay_recv, pass_send, pass_recv, load_sem, move_send, move_recv, raw_send, raw_recv, turn_send, turn_recv, swap_send, swap_recv, sum_send, sum_recv, quad_send, quad_recv, rot_send, rot_recv, whole_send, whole_recv,
):
    slots, rows, _ = cur.shape
    size = 2 * W
    chunk = rows // CHUNKS
    chips = members // 2
    stages = chips.bit_length() - 1
    g = lax.axis_index("col")
    m = lax.axis_index("row")
    core = lax.rem(m, 2)
    chip = m // 2
    partner = m + 1 - 2 * core
    half = g // 2
    at_end = jnp.logical_or(g == 0, g == groups - 1)
    inside = jnp.logical_not(at_end)
    goals = [2 - half, g + 1 - 2 * lax.rem(g, 2), 3 - 3 * half]

    def flipped(bit):
        step = 1 << bit
        on = lax.rem(chip // step, 2)
        return (chip + step - 2 * step * on) * 2 + core

    loads = []
    for q in range(CHUNKS):
        span = pl.ds(q * chunk, chunk)
        loads.append(pltpu.make_async_copy(factor_ref.at[span], held.at[span], load_sem.at[q]))
        loads[q].start()

    goal_peers = [{"col": goal, "row": m} for goal in goals]
    row_peers = [{"col": g, "row": partner}]
    row_peers += [{"col": g, "row": flipped(b)} for b in range(stages)]
    quads = stages // 2
    quad_peers = []
    for b in range(quads):
        one, two = flipped(b), flipped(b + quads)
        quad_peers.append([{"col": g, "row": other} for other in (one, two, one + two - m)])
    diagonals = [quad[2] for quad in quad_peers]
    barrier = pltpu.get_barrier_semaphore()
    for peer in goal_peers + row_peers + diagonals:
        pl.semaphore_signal(barrier, inc=1, device_id=peer, device_id_type=MESH)

    row_ids = lax.broadcasted_iota(jnp.int32, (size, size), 0)
    col_ids = lax.broadcasted_iota(jnp.int32, (size, size), 1)
    eye = (row_ids == col_ids).astype(F32)

    def mask(q):
        loads[q].wait()
        for s in range(slots):
            for b in range(q * chunk // RB, (q + 1) * chunk // RB):
                span = pl.ds(b * RB, RB)
                weight = support_ref[b, g * slots + s].astype(F32)
                cur[s, span] = held[span, s * W:(s + 1) * W] * weight

    def before(r, position):
        return position if r == 0 else plan_ref[r - 1, position]

    blocks = groups * slots
    pick, keep, take = [], [], []
    for r in range(ROUNDS):
        dest = []
        for s in range(slots):
            block = before(r, g * slots + s)
            dest.append(sum(
                jnp.where(plan_ref[r, j] == block, j // slots, 0) for j in range(blocks)))

        def slot_for(goal):
            return jnp.minimum(slots - 1, sum(
                jnp.where(dest[s] == goal, s, 0) for s in range(slots)))

        pick.append([slot_for(goal) for goal in goals])
        keep.append(slot_for(g))
        take.append([])
        for s in range(slots):
            block = plan_ref[r, g * slots + s]
            take[r].append(jnp.minimum(groups - 1, sum(
                jnp.where(before(r, j) == block, j // slots, 0) for j in range(blocks))))

    copies = []

    def start(copy):
        copy.start()
        copies.append(copy)
        return copy

    def move(r, q, j, source, last=False):
        count = chunk - RELAY if last and q == CHUNKS - 1 else chunk
        landing = late[q] if last else recv[r][q].at[source]
        return pltpu.make_async_remote_copy(
            src_ref=send.at[r, j, pl.ds(q * chunk, count)],
            dst_ref=landing.at[pl.ds(0, count)],
            send_sem=move_send.at[r, q, j],
            recv_sem=move_recv.at[r, q, source],
            device_id=goal_peers[j],
            device_id_type=MESH,
        )

    across = (0, groups - 2)
    relays = [pltpu.make_async_remote_copy(
        src_ref=send.at[1, j, pl.ds(rows - RELAY, RELAY)],
        dst_ref=relay.at[i],
        send_sem=relay_send.at[i],
        recv_sem=relay_recv.at[i],
        device_id=goal_peers[1],
        device_id_type=MESH,
    ) for i, j in enumerate(across)]
    passes = [pltpu.make_async_remote_copy(
        src_ref=relay.at[i],
        dst_ref=late[CHUNKS - 1].at[pl.ds(chunk - RELAY, RELAY)],
        send_sem=pass_send.at[i],
        recv_sem=pass_recv.at[0],
        device_id=goal_peers[j],
        device_id_type=MESH,
    ) for i, j in enumerate(across)]

    def prepare(r, q):
        span = pl.ds(q * chunk, chunk)
        for j in range(groups - 1):
            send[r, j, span] = cur[pick[r][j], span]
        recv[r][q][g] = cur[keep[r], span]

    def arrive_first(q):
        for source in goals:
            move(0, q, 0, source).wait_recv()

    def arrive_early(q):
        move(1, q, 0, goals[0]).wait_recv()

        @pl.when(at_end)
        def _():
            move(1, q, 0, goals[1]).wait_recv()

    def arrive_late(q):
        move(1, q, 0, goals[2], True).wait_recv()
        if q == CHUNKS - 1:
            passes[0].wait_recv()

    raws = [pltpu.make_async_remote_copy(
        src_ref=raw_out.at[q],
        dst_ref=raw_in.at[q],
        send_sem=raw_send.at[q],
        recv_sem=raw_recv.at[q],
        device_id=goal_peers[1],
        device_id_type=MESH,
    ) for q in range(CHUNKS)]
    near_slot = pick[1][1]
    share = pl.ds(pl.multiple_of(core * W, W), W)
    turn_copy = pltpu.make_async_remote_copy(
        src_ref=turn_out,
        dst_ref=turn.at[share],
        send_sem=turn_send.at[0],
        recv_sem=turn_recv.at[0],
        device_id=goal_peers[1],
        device_id_type=MESH,
    )
    turn_swap = pltpu.make_async_remote_copy(
        src_ref=turn.at[share],
        dst_ref=turn.at[share],
        send_sem=turn_send.at[1],
        recv_sem=turn_recv.at[1],
        device_id=row_peers[0],
        device_id_type=MESH,
    )

    def start_raw(q):
        @pl.when(at_end)
        def _():
            raw_out[q] = load_pair(near_slot // 2, q)
            raws[q].start()

    def start_turn():
        @pl.when(at_end)
        def _():
            side = jnp.where(near_slot // 2 == core, 0, 1)
            wide = rot[side, share]
            turn_out[...] = jnp.where(lax.rem(near_slot, 2) == 0, wide[:, :W], wide[:, W:])
            turn_copy.start()

    def turn_raws():
        @pl.when(inside)
        def _():
            turn_copy.wait_recv()
            turn_swap.start()
            turn_swap.wait_recv()
            for q in range(CHUNKS):
                raws[q].wait_recv()
                recv[1][q][goals[1]] = dot3(raw_in[q], turn[...])

    def start_second(q):
        @pl.when(inside)
        def _():
            for j in (*across, 1):
                move(1, q, j, g).start()

        if q == CHUNKS - 1:
            @pl.when(at_end)
            def _():
                for copy in relays:
                    copy.start()

    def start_far():
        @pl.when(inside)
        def _():
            for q in range(CHUNKS):
                for j in across:
                    move(1, q, j, g).wait_send()
            pl.semaphore_signal(go_sem.at[1], inc=1, device_id=goal_peers[1], device_id_type=MESH)
            for i in range(2):
                relays[i].wait_recv()
                passes[i].start()

        @pl.when(at_end)
        def _():
            pl.semaphore_wait(go_sem.at[1], 1)
            for q in range(CHUNKS):
                for j in across:
                    move(1, q, j, g, True).start()

    def load_pair(k, q):
        first = jnp.where(k == 0, take[0][0], take[0][2])
        last = jnp.where(k == 0, take[0][1], take[0][3])
        return jnp.concatenate([recv[0][q][first], recv[0][q][last]], axis=1)

    far = goals[2]
    late_last = jnp.logical_or(take[1][2] == far, take[1][3] == far)
    late_pair = [jnp.where(late_last, take[1][2 + i], take[1][i]) for i in range(2)]
    early_pair = [jnp.where(late_last, take[1][i], take[1][2 + i]) for i in range(2)]
    far_left = late_pair[0] == far
    late_other = jnp.where(far_left, late_pair[1], late_pair[0])

    def load_early(q):
        return jnp.concatenate([recv[1][q][block] for block in early_pair], axis=1)

    def load_late(q):
        newest, other = late[q][...], recv[1][q][late_other]
        left, right = jnp.where(far_left, newest, other), jnp.where(far_left, other, newest)
        return jnp.concatenate([left, right], axis=1)

    def add_gram(k, q, pair):
        high, low = split(pair)
        mixed = dot_t(high, low)
        part = dot_t(high, high) + (mixed + mixed.T)
        acc[k] = part if q == 0 else acc[k] + part

    def sum_chips(total, slots_ref, cut):
        for stage in range(stages):
            slots_ref[2 * stage] = total
            both = []
            for h in range(2):
                bit = (stage + h * (stages // 2)) % stages
                part = pl.ds(0, cut) if h == 0 else pl.ds(cut, total.shape[0] - cut)
                both.append(start(pltpu.make_async_remote_copy(
                    src_ref=slots_ref.at[2 * stage, part],
                    dst_ref=slots_ref.at[2 * stage + 1, part],
                    send_sem=sum_send.at[stage, h],
                    recv_sem=sum_recv.at[stage, h],
                    device_id=row_peers[1 + bit],
                    device_id_type=MESH,
                )))
            for copy in both:
                copy.wait_recv()
            total = total + slots_ref[2 * stage + 1]
        return total

    def sum_quads(e, total):
        for step in range(quads):
            piece[e, 4 * step] = total
            three = [start(pltpu.make_async_remote_copy(
                src_ref=piece.at[e, 4 * step],
                dst_ref=piece.at[e, 4 * step + 1 + i],
                send_sem=quad_send.at[e, step, i],
                recv_sem=quad_recv.at[e, step, i],
                device_id=quad_peers[step][i],
                device_id_type=MESH,
            )) for i in (2, 0, 1)]
            for copy in three:
                copy.wait_recv()
            pair, other = (piece[e, 4 * step + 2 * i] + piece[e, 4 * step + 2 * i + 1] for i in range(2))
            total = pair + other
        return total

    def rotation_of(e):
        cross, tile, diagonal = pack(acc[e])
        piece_in[e, 0, :W] = cross
        piece_in[e, 0, W:] = diagonal
        piece_in[e, 1, :W] = tile
        piece_in[e, 1, W:] = diagonal
        start(pltpu.make_async_remote_copy(
            src_ref=piece_in.at[e, 1 - core],
            dst_ref=piece_in.at[e, 2],
            send_sem=swap_send.at[1 + e],
            recv_sem=swap_recv.at[1 + e],
            device_id=row_peers[0],
            device_id_type=MESH,
        )).wait_recv()
        total = sum_quads(e, piece_in[e, core] + piece_in[e, 2])
        whole[e, core] = total
        start(pltpu.make_async_remote_copy(
            src_ref=whole.at[e, core],
            dst_ref=whole.at[e, core],
            send_sem=whole_send.at[e],
            recv_sem=whole_recv.at[e],
            device_id=row_peers[0],
            device_id_type=MESH,
        )).wait_recv()
        return rotation(unpack(whole[e, 0, :W], whole[e, 1, :W], whole[e, 0, W:W + 1]), eye, stack)

    mask(0)
    prepare(0, 0)
    pl.semaphore_wait(barrier, groups - 1 + len(row_peers) + quads)
    for q in range(CHUNKS):
        if q:
            mask(q)
            prepare(0, q)
        for j in range(groups - 2):
            start(move(0, q, j, g))
    @pl.when(at_end)
    def _():
        pl.semaphore_wait(go_sem.at[0], 1)
        for q in range(CHUNKS):
            move(0, q, groups - 2, g).start()

    for q in range(CHUNKS):
        arrive_first(q)
        if q == CHUNKS - 2:
            @pl.when(inside)
            def _():
                for c in range(CHUNKS):
                    move(0, c, groups - 2, g).start()
        if q == CHUNKS - 1:
            @pl.when(inside)
            def _():
                pl.semaphore_signal(go_sem.at[0], inc=1, device_id=goal_peers[1], device_id_type=MESH)
        start_raw(q)
        for k in range(2):
            add_gram(k, q, load_pair(k, q))
    for k in range(2):
        cross, tile, diagonal = pack(acc[k])
        gram_in[k, :W] = cross
        gram_in[k, W:size] = tile
        gram_in[k, size:] = diagonal
    start(pltpu.make_async_remote_copy(
        src_ref=gram_in.at[1 - core],
        dst_ref=gram_in.at[2],
        send_sem=swap_send.at[0],
        recv_sem=swap_recv.at[0],
        device_id=row_peers[0],
        device_id_type=MESH,
    )).wait_recv()
    total = sum_chips(gram_in[core] + gram_in[2], gram, W)
    rot[0] = rotation(unpack(total[:W], total[W:size], total[size:size + 1]), eye, stack)
    back = start(pltpu.make_async_remote_copy(
        src_ref=rot.at[0],
        dst_ref=rot.at[1],
        send_sem=rot_send.at[0],
        recv_sem=rot_recv.at[0],
        device_id=row_peers[0],
        device_id_type=MESH,
    ))
    for side in range(2):
        k = core if side == 0 else 1 - core
        if side == 1:
            back.wait_recv()
        for q in (CHUNKS - 1, *range(CHUNKS - 1)):
            span = pl.ds(q * chunk, chunk)
            turned = dot3(load_pair(k, q), rot[side])
            cur[2 * k, span] = turned[:, :W]
            cur[2 * k + 1, span] = turned[:, W:]
            if side == 1:
                prepare(1, q)
                start_second(q)
                if q == CHUNKS - 1:
                    start_turn()

    start_far()
    turn_raws()
    for q in range(CHUNKS):
        arrive_early(q)
        add_gram(0, q, load_early(q))
    early = rotation_of(0)
    for q in range(CHUNKS):
        held[pl.ds(q * chunk, chunk), :size] = dot3(load_early(q), early)
    for q in range(CHUNKS):
        arrive_late(q)
        add_gram(1, q, load_late(q))
    last = rotation_of(1)
    for q in range(CHUNKS):
        span = pl.ds(q * chunk, chunk)
        turned, ready = dot3(load_late(q), last), held[span, :size]
        out_ref[span, :size] = jnp.where(late_last, ready, turned)
        out_ref[span, size:] = jnp.where(late_last, turned, ready)
    @pl.when(at_end)
    def _():
        for copy in [*raws, turn_copy]:
            copy.wait_send()

    @pl.when(inside)
    def _():
        turn_swap.wait_send()
        for copy in passes:
            copy.wait_send()
        for q in range(CHUNKS):
            move(1, q, 1, g).wait_send()

    for q in range(CHUNKS):
        move(0, q, groups - 2, g).wait_send()

    @pl.when(at_end)
    def _():
        for q in range(CHUNKS):
            for j in across:
                move(1, q, j, g, True).wait_send()
        for copy in relays:
            copy.wait_send()

    for copy in copies:
        copy.wait_send()


def on_device(groups, members, factor, support, plan):
    rows = factor.shape[0]
    slots = factor.shape[1] // W
    chips = members // 2
    stages = chips.bit_length() - 1
    assert slots == 4 and groups == 4 and chips == 1 << stages and stages % 2 == 0 and ROUNDS == 2
    size = 2 * W
    dma = pltpu.SemaphoreType.DMA
    smem = pl.BlockSpec(memory_space=pltpu.SMEM)
    return pl.pallas_call(
        functools.partial(kernel, groups, members),
        out_shape=jax.ShapeDtypeStruct(factor.shape, F32),
        in_specs=[pl.BlockSpec(memory_space=pl.ANY), smem, smem],
        out_specs=pl.BlockSpec(memory_space=pltpu.VMEM),
        scratch_shapes=[
            pltpu.VMEM(factor.shape, F32),
            pltpu.VMEM((slots, rows, W), F32),
            pltpu.VMEM((ROUNDS, groups - 1, rows, W), F32),
            [[pltpu.VMEM((groups, rows // CHUNKS, W), F32)] * CHUNKS] * ROUNDS,
            [pltpu.VMEM((rows // CHUNKS, W), F32)] * CHUNKS,
            pltpu.VMEM((2, RELAY, W), F32),
            pltpu.VMEM((CHUNKS, rows // CHUNKS, size), F32),
            pltpu.VMEM((CHUNKS, rows // CHUNKS, size), F32),
            pltpu.VMEM((W, W), F32),
            pltpu.VMEM((size, W), F32),
            pltpu.VMEM((2, size, size), F32),
            pltpu.VMEM((2 * stages, size + 8, W), F32),
            pltpu.VMEM((3, size + 8, W), F32),
            pltpu.VMEM((2, 2 * stages, W + 8, W), F32),
            pltpu.VMEM((2, 3, W + 8, W), F32),
            pltpu.VMEM((2, 2, W + 8, W), F32),
            pltpu.VMEM((2, size, size), F32),
            pltpu.VMEM((2 * size, size), F32),
            pltpu.SemaphoreType.REGULAR((2,)),
            dma((2,)),
            dma((2,)),
            dma((2,)),
            dma((1,)),
            dma((CHUNKS,)),
            dma((ROUNDS, CHUNKS, groups - 1)),
            dma((ROUNDS, CHUNKS, groups)),
            dma((CHUNKS,)),
            dma((CHUNKS,)),
            dma((2,)),
            dma((2,)),
            dma((3,)),
            dma((3,)),
            dma((stages, 2)),
            dma((stages, 2)),
            dma((2, stages // 2, 3)),
            dma((2, stages // 2, 3)),
            dma((1,)),
            dma((1,)),
            dma((2,)),
            dma((2,)),
        ],
        compiler_params=pltpu.CompilerParams(
            collective_id=0, has_side_effects=True, vmem_limit_bytes=30 * 1024 * 1024
        ),
    )(*(pltpu.with_memory_space_constraint(x, pltpu.HBM) for x in (factor, support.T, plan)))


def solution(mesh):
    return jax.shard_map(
        functools.partial(on_device, mesh.shape["col"], mesh.shape["row"]),
        mesh=mesh,
        in_specs=(P("row", "col"), P(None, "row"), P()),
        out_specs=P("row", "col"),
        check_vma=False,
    )
```

```python
import functools

import jax
import jax.numpy as jnp
from jax import lax
from jax.experimental import pallas as pl
from jax.experimental.pallas import tpu as pltpu
from jax.sharding import PartitionSpec as P

W = 128
RB = 128
ROUNDS = 2
CHUNKS = 4
STEPS = 7
DAMPING = 0.01
RELAY = 160
TOP = 2020.0
F32 = jnp.float32
BF16 = jnp.bfloat16
MESH = pl.DeviceIdType.MESH


def split(x):
    high = x.astype(BF16)
    return high, (x - high.astype(F32)).astype(BF16)


def dot(a, b):
    return jnp.dot(a, b, preferred_element_type=F32)


def dot3(a, b):
    a_high, a_low = split(a)
    b_high, b_low = split(b)
    return dot(a_high, b_high) + (dot(a_high, b_low) + dot(a_low, b_high))


def dot_t(a, b):
    return lax.dot_general(a, b, (((0,), (0,)), ((), ())), preferred_element_type=F32)


def rotation(gram, eye, stack):
    size = gram.shape[0]
    on_diagonal = gram * eye
    diag_rows = jnp.sum(on_diagonal, axis=1, keepdims=True)
    diag_cols = jnp.sum(on_diagonal, axis=0, keepdims=True)
    spread = diag_rows - diag_cols
    joined = diag_rows + diag_cols
    half = 0.5 * gram * spread / (spread * spread + gram * gram + DAMPING * joined * joined)
    squared = dot3(half, half)
    stack[:size] = eye - squared
    stack[size:] = eye - half
    scales, low, high = [], 1.0, TOP
    for _ in range(STEPS):
        scales.append(2.0 / (low + high))
        low, high = 4.0 * low * high / (low + high) ** 2, 1.0

    def factor(scale):
        return (2.0 * scale) * eye - (scale * scale) * stack[:size]

    def scaled(step, carry):
        scale = jnp.float32(scales[0])
        for i in range(1, STEPS - 1):
            scale = jnp.where(step == i, scales[i], scale)
        stack[...] = dot3(stack[...], factor(scale))
        return carry

    lax.fori_loop(0, STEPS - 1, scaled, 0)
    inverse = dot3(stack[size:], factor(scales[-1]))
    residual = (eye - inverse) - dot3(half, inverse)
    short = residual.astype(BF16)
    inverse = inverse + dot3(inverse, residual + dot(short, short))
    return 2.0 * inverse - eye


def pack(gram):
    first, last = gram[:W, :W], gram[W:, W:]
    row_ids = lax.broadcasted_iota(jnp.int32, (W, W), 0)
    col_ids = lax.broadcasted_iota(jnp.int32, (W, W), 1)
    tile = jnp.where(row_ids >= col_ids, first, last)
    diagonal = jnp.sum(jnp.where(row_ids == col_ids, last, 0.0), axis=0, keepdims=True)
    return gram[:W, W:], tile, jnp.broadcast_to(diagonal, (8, W))


def unpack(cross, tile, diagonal):
    row_ids = lax.broadcasted_iota(jnp.int32, (W, W), 0)
    col_ids = lax.broadcasted_iota(jnp.int32, (W, W), 1)
    lower = jnp.where(row_ids > col_ids, tile, 0.0)
    upper = jnp.where(row_ids < col_ids, tile, 0.0)
    first = lower + lower.T + jnp.where(row_ids == col_ids, tile, 0.0)
    last = upper + upper.T + jnp.where(row_ids == col_ids, diagonal, 0.0)
    top = jnp.concatenate([first, cross], axis=1)
    return jnp.concatenate([top, jnp.concatenate([cross.T, last], axis=1)], axis=0)


def kernel(
    groups, members, factor_ref, support_ref, plan_ref, out_ref,
    held, cur, send, recv, late, relay, halves, raw_out, raw_in, turn_out, turn, acc, gram, gram_in,
    piece, piece_in, whole, rot, stack,
    go_sem, relay_send, relay_recv, pass_send, pass_recv, load_sem, move_send, move_recv, raw_send, raw_recv, turn_send, turn_recv, swap_send, swap_recv, sum_send, sum_recv, quad_send, quad_recv, rot_send, rot_recv, whole_send, whole_recv,
):
    slots, rows, _ = cur.shape
    size = 2 * W
    chunk = rows // CHUNKS
    chips = members // 2
    stages = chips.bit_length() - 1
    g = lax.axis_index("col")
    m = lax.axis_index("row")
    core = lax.rem(m, 2)
    chip = m // 2
    partner = m + 1 - 2 * core
    half = g // 2
    at_end = jnp.logical_or(g == 0, g == groups - 1)
    inside = jnp.logical_not(at_end)
    goals = [2 - half, g + 1 - 2 * lax.rem(g, 2), 3 - 3 * half]

    def flipped(bit):
        step = 1 << bit
        on = lax.rem(chip // step, 2)
        return (chip + step - 2 * step * on) * 2 + core

    loads = []
    for q in range(CHUNKS):
        span = pl.ds(q * chunk, chunk)
        loads.append(pltpu.make_async_copy(factor_ref.at[span], held.at[span], load_sem.at[q]))
        loads[q].start()

    goal_peers = [{"col": goal, "row": m} for goal in goals]
    row_peers = [{"col": g, "row": partner}]
    row_peers += [{"col": g, "row": flipped(b)} for b in range(stages)]
    quads = stages // 2
    quad_peers = []
    for b in range(quads):
        one, two = flipped(b), flipped(b + quads)
        quad_peers.append([{"col": g, "row": other} for other in (one, two, one + two - m)])
    diagonals = [quad[2] for quad in quad_peers]
    barrier = pltpu.get_barrier_semaphore()
    for peer in goal_peers + row_peers + diagonals:
        pl.semaphore_signal(barrier, inc=1, device_id=peer, device_id_type=MESH)

    row_ids = lax.broadcasted_iota(jnp.int32, (size, size), 0)
    col_ids = lax.broadcasted_iota(jnp.int32, (size, size), 1)
    eye = (row_ids == col_ids).astype(F32)

    def mask(q):
        loads[q].wait()
        for s in range(slots):
            for b in range(q * chunk // RB, (q + 1) * chunk // RB):
                span = pl.ds(b * RB, RB)
                weight = support_ref[b, g * slots + s].astype(F32)
                cur[s, span] = held[span, s * W:(s + 1) * W] * weight

    def before(r, position):
        return position if r == 0 else plan_ref[r - 1, position]

    blocks = groups * slots
    pick, keep, take = [], [], []
    for r in range(ROUNDS):
        dest = []
        for s in range(slots):
            block = before(r, g * slots + s)
            dest.append(sum(
                jnp.where(plan_ref[r, j] == block, j // slots, 0) for j in range(blocks)))

        def slot_for(goal):
            return jnp.minimum(slots - 1, sum(
                jnp.where(dest[s] == goal, s, 0) for s in range(slots)))

        pick.append([slot_for(goal) for goal in goals])
        keep.append(slot_for(g))
        take.append([])
        for s in range(slots):
            block = plan_ref[r, g * slots + s]
            take[r].append(jnp.minimum(groups - 1, sum(
                jnp.where(before(r, j) == block, j // slots, 0) for j in range(blocks))))

    copies = []

    def start(copy):
        copy.start()
        copies.append(copy)
        return copy

    def move(r, q, j, source, last=False):
        count = chunk - RELAY if last and q == CHUNKS - 1 else chunk
        landing = late[q] if last else recv[r][q].at[source]
        return pltpu.make_async_remote_copy(
            src_ref=send.at[r, j, pl.ds(q * chunk, count)],
            dst_ref=landing.at[pl.ds(0, count)],
            send_sem=move_send.at[r, q, j],
            recv_sem=move_recv.at[r, q, source],
            device_id=goal_peers[j],
            device_id_type=MESH,
        )

    across = (0, groups - 2)
    relays = [pltpu.make_async_remote_copy(
        src_ref=send.at[1, j, pl.ds(rows - RELAY, RELAY)],
        dst_ref=relay.at[i],
        send_sem=relay_send.at[i],
        recv_sem=relay_recv.at[i],
        device_id=goal_peers[1],
        device_id_type=MESH,
    ) for i, j in enumerate(across)]
    passes = [pltpu.make_async_remote_copy(
        src_ref=relay.at[i],
        dst_ref=late[CHUNKS - 1].at[pl.ds(chunk - RELAY, RELAY)],
        send_sem=pass_send.at[i],
        recv_sem=pass_recv.at[0],
        device_id=goal_peers[j],
        device_id_type=MESH,
    ) for i, j in enumerate(across)]

    def prepare(r, q):
        span = pl.ds(q * chunk, chunk)
        for j in range(groups - 1):
            send[r, j, span] = cur[pick[r][j], span]
        recv[r][q][g] = cur[keep[r], span]

    def arrive_first(q):
        for source in goals:
            move(0, q, 0, source).wait_recv()

    def arrive_early(q):
        move(1, q, 0, goals[0]).wait_recv()

        @pl.when(at_end)
        def _():
            move(1, q, 0, goals[1]).wait_recv()

    def arrive_late(q):
        move(1, q, 0, goals[2], True).wait_recv()
        if q == CHUNKS - 1:
            passes[0].wait_recv()

    raws = [pltpu.make_async_remote_copy(
        src_ref=raw_out.at[q],
        dst_ref=raw_in.at[q],
        send_sem=raw_send.at[q],
        recv_sem=raw_recv.at[q],
        device_id=goal_peers[1],
        device_id_type=MESH,
    ) for q in range(CHUNKS)]
    near_slot = pick[1][1]
    share = pl.ds(pl.multiple_of(core * W, W), W)
    turn_copy = pltpu.make_async_remote_copy(
        src_ref=turn_out,
        dst_ref=turn.at[share],
        send_sem=turn_send.at[0],
        recv_sem=turn_recv.at[0],
        device_id=goal_peers[1],
        device_id_type=MESH,
    )
    turn_swap = pltpu.make_async_remote_copy(
        src_ref=turn.at[share],
        dst_ref=turn.at[share],
        send_sem=turn_send.at[1],
        recv_sem=turn_recv.at[1],
        device_id=row_peers[0],
        device_id_type=MESH,
    )

    def start_raw(q):
        @pl.when(at_end)
        def _():
            raw_out[q] = load_pair(near_slot // 2, q)
            raws[q].start()

    def start_turn():
        @pl.when(at_end)
        def _():
            side = jnp.where(near_slot // 2 == core, 0, 1)
            wide = rot[side, share]
            turn_out[...] = jnp.where(lax.rem(near_slot, 2) == 0, wide[:, :W], wide[:, W:])
            turn_copy.start()

    def turn_raws():
        @pl.when(inside)
        def _():
            turn_copy.wait_recv()
            turn_swap.start()
            turn_swap.wait_recv()
            for q in range(CHUNKS):
                raws[q].wait_recv()
                recv[1][q][goals[1]] = dot3(raw_in[q], turn[...])

    def start_second(q):
        @pl.when(inside)
        def _():
            for j in (*across, 1):
                move(1, q, j, g).start()

        if q == CHUNKS - 1:
            @pl.when(at_end)
            def _():
                for copy in relays:
                    copy.start()

    def start_far():
        @pl.when(inside)
        def _():
            for q in range(CHUNKS):
                for j in across:
                    move(1, q, j, g).wait_send()
            pl.semaphore_signal(go_sem.at[1], inc=1, device_id=goal_peers[1], device_id_type=MESH)
            for i in range(2):
                relays[i].wait_recv()
                passes[i].start()

        @pl.when(at_end)
        def _():
            pl.semaphore_wait(go_sem.at[1], 1)
            for q in range(CHUNKS):
                for j in across:
                    move(1, q, j, g, True).start()

    def load_pair(k, q):
        first = jnp.where(k == 0, take[0][0], take[0][2])
        last = jnp.where(k == 0, take[0][1], take[0][3])
        return jnp.concatenate([recv[0][q][first], recv[0][q][last]], axis=1)

    far = goals[2]
    late_last = jnp.logical_or(take[1][2] == far, take[1][3] == far)
    late_pair = [jnp.where(late_last, take[1][2 + i], take[1][i]) for i in range(2)]
    early_pair = [jnp.where(late_last, take[1][i], take[1][2 + i]) for i in range(2)]
    far_left = late_pair[0] == far
    late_other = jnp.where(far_left, late_pair[1], late_pair[0])

    def load_early(q):
        return jnp.concatenate([recv[1][q][block] for block in early_pair], axis=1)

    def load_late(q):
        newest, other = late[q][...], recv[1][q][late_other]
        left, right = jnp.where(far_left, newest, other), jnp.where(far_left, other, newest)
        return jnp.concatenate([left, right], axis=1)

    def add_gram(k, q, pair):
        high, low = split(pair)
        mixed = dot_t(high, low)
        part = dot_t(high, high) + (mixed + mixed.T)
        acc[k] = part if q == 0 else acc[k] + part

    def sum_chips(total, slots_ref, cut):
        for stage in range(stages):
            slots_ref[2 * stage] = total
            both = []
            for h in range(2):
                bit = (stage + h * (stages // 2)) % stages
                part = pl.ds(0, cut) if h == 0 else pl.ds(cut, total.shape[0] - cut)
                both.append(start(pltpu.make_async_remote_copy(
                    src_ref=slots_ref.at[2 * stage, part],
                    dst_ref=slots_ref.at[2 * stage + 1, part],
                    send_sem=sum_send.at[stage, h],
                    recv_sem=sum_recv.at[stage, h],
                    device_id=row_peers[1 + bit],
                    device_id_type=MESH,
                )))
            for copy in both:
                copy.wait_recv()
            total = total + slots_ref[2 * stage + 1]
        return total

    def sum_quads(e, total):
        for step in range(quads):
            piece[e, 4 * step] = total
            three = [start(pltpu.make_async_remote_copy(
                src_ref=piece.at[e, 4 * step],
                dst_ref=piece.at[e, 4 * step + 1 + i],
                send_sem=quad_send.at[e, step, i],
                recv_sem=quad_recv.at[e, step, i],
                device_id=quad_peers[step][i],
                device_id_type=MESH,
            )) for i in (2, 0, 1)]
            for copy in three:
                copy.wait_recv()
            pair, other = (piece[e, 4 * step + 2 * i] + piece[e, 4 * step + 2 * i + 1] for i in range(2))
            total = pair + other
        return total

    def rotation_of(e):
        cross, tile, diagonal = pack(acc[e])
        piece_in[e, 0, :W] = cross
        piece_in[e, 0, W:] = diagonal
        piece_in[e, 1, :W] = tile
        piece_in[e, 1, W:] = diagonal
        start(pltpu.make_async_remote_copy(
            src_ref=piece_in.at[e, 1 - core],
            dst_ref=piece_in.at[e, 2],
            send_sem=swap_send.at[1 + e],
            recv_sem=swap_recv.at[1 + e],
            device_id=row_peers[0],
            device_id_type=MESH,
        )).wait_recv()
        total = sum_quads(e, piece_in[e, core] + piece_in[e, 2])
        whole[e, core] = total
        start(pltpu.make_async_remote_copy(
            src_ref=whole.at[e, core],
            dst_ref=whole.at[e, core],
            send_sem=whole_send.at[e],
            recv_sem=whole_recv.at[e],
            device_id=row_peers[0],
            device_id_type=MESH,
        )).wait_recv()
        return rotation(unpack(whole[e, 0, :W], whole[e, 1, :W], whole[e, 0, W:W + 1]), eye, stack)

    mask(0)
    prepare(0, 0)
    pl.semaphore_wait(barrier, groups - 1 + len(row_peers) + quads)
    for q in range(CHUNKS):
        if q:
            mask(q)
            prepare(0, q)
        for j in range(groups - 2):
            start(move(0, q, j, g))
    @pl.when(at_end)
    def _():
        pl.semaphore_wait(go_sem.at[0], 1)
        for q in range(CHUNKS):
            move(0, q, groups - 2, g).start()

    for q in range(CHUNKS):
        arrive_first(q)
        if q == CHUNKS - 2:
            @pl.when(inside)
            def _():
                for c in range(CHUNKS):
                    move(0, c, groups - 2, g).start()
        if q == CHUNKS - 1:
            @pl.when(inside)
            def _():
                pl.semaphore_signal(go_sem.at[0], inc=1, device_id=goal_peers[1], device_id_type=MESH)
        start_raw(q)
        for k in range(2):
            add_gram(k, q, load_pair(k, q))
    for k in range(2):
        cross, tile, diagonal = pack(acc[k])
        gram_in[k, :W] = cross
        gram_in[k, W:size] = tile
        gram_in[k, size:] = diagonal
    start(pltpu.make_async_remote_copy(
        src_ref=gram_in.at[1 - core],
        dst_ref=gram_in.at[2],
        send_sem=swap_send.at[0],
        recv_sem=swap_recv.at[0],
        device_id=row_peers[0],
        device_id_type=MESH,
    )).wait_recv()
    total = sum_chips(gram_in[core] + gram_in[2], gram, W)
    rot[0] = rotation(unpack(total[:W], total[W:size], total[size:size + 1]), eye, stack)
    back = start(pltpu.make_async_remote_copy(
        src_ref=rot.at[0],
        dst_ref=rot.at[1],
        send_sem=rot_send.at[0],
        recv_sem=rot_recv.at[0],
        device_id=row_peers[0],
        device_id_type=MESH,
    ))
    for side in range(2):
        k = core if side == 0 else 1 - core
        if side == 1:
            back.wait_recv()
        for q in (CHUNKS - 1, *range(CHUNKS - 1)):
            span = pl.ds(q * chunk, chunk)
            turned = dot3(load_pair(k, q), rot[side])
            cur[2 * k, span] = turned[:, :W]
            cur[2 * k + 1, span] = turned[:, W:]
            if side == 1:
                prepare(1, q)
                start_second(q)
                if q == CHUNKS - 1:
                    start_turn()

    start_far()
    turn_raws()
    for q in range(CHUNKS):
        arrive_early(q)
        add_gram(0, q, load_early(q))
    early = rotation_of(0)
    for q in range(CHUNKS):
        held[pl.ds(q * chunk, chunk), :size] = dot3(load_early(q), early)
    for q in range(CHUNKS):
        arrive_late(q)
        pair = load_late(q)
        add_gram(1, q, pair)
        halves[0, q], halves[1, q] = split(pair)
    last_high, last_low = split(rotation_of(1))
    for q in range(CHUNKS):
        span = pl.ds(q * chunk, chunk)
        high, low, ready = halves[0, q], halves[1, q], held[span, :size]
        turned = dot(high, last_high) + (dot(high, last_low) + dot(low, last_high))
        out_ref[span, :size] = jnp.where(late_last, ready, turned)
        out_ref[span, size:] = jnp.where(late_last, turned, ready)
    @pl.when(at_end)
    def _():
        for copy in [*raws, turn_copy]:
            copy.wait_send()

    @pl.when(inside)
    def _():
        turn_swap.wait_send()
        for copy in passes:
            copy.wait_send()
        for q in range(CHUNKS):
            move(1, q, 1, g).wait_send()

    for q in range(CHUNKS):
        move(0, q, groups - 2, g).wait_send()

    @pl.when(at_end)
    def _():
        for q in range(CHUNKS):
            for j in across:
                move(1, q, j, g, True).wait_send()
        for copy in relays:
            copy.wait_send()

    for copy in copies:
        copy.wait_send()


def on_device(groups, members, factor, support, plan):
    rows = factor.shape[0]
    slots = factor.shape[1] // W
    chips = members // 2
    stages = chips.bit_length() - 1
    assert slots == 4 and groups == 4 and chips == 1 << stages and stages % 2 == 0 and ROUNDS == 2
    size = 2 * W
    dma = pltpu.SemaphoreType.DMA
    smem = pl.BlockSpec(memory_space=pltpu.SMEM)
    return pl.pallas_call(
        functools.partial(kernel, groups, members),
        out_shape=jax.ShapeDtypeStruct(factor.shape, F32),
        in_specs=[pl.BlockSpec(memory_space=pl.ANY), smem, smem],
        out_specs=pl.BlockSpec(memory_space=pltpu.VMEM),
        scratch_shapes=[
            pltpu.VMEM(factor.shape, F32),
            pltpu.VMEM((slots, rows, W), F32),
            pltpu.VMEM((ROUNDS, groups - 1, rows, W), F32),
            [[pltpu.VMEM((groups, rows // CHUNKS, W), F32)] * CHUNKS] * ROUNDS,
            [pltpu.VMEM((rows // CHUNKS, W), F32)] * CHUNKS,
            pltpu.VMEM((2, RELAY, W), F32),
            pltpu.VMEM((2, CHUNKS, rows // CHUNKS, size), BF16),
            pltpu.VMEM((CHUNKS, rows // CHUNKS, size), F32),
            pltpu.VMEM((CHUNKS, rows // CHUNKS, size), F32),
            pltpu.VMEM((W, W), F32),
            pltpu.VMEM((size, W), F32),
            pltpu.VMEM((2, size, size), F32),
            pltpu.VMEM((2 * stages, size + 8, W), F32),
            pltpu.VMEM((3, size + 8, W), F32),
            pltpu.VMEM((2, 2 * stages, W + 8, W), F32),
            pltpu.VMEM((2, 3, W + 8, W), F32),
            pltpu.VMEM((2, 2, W + 8, W), F32),
            pltpu.VMEM((2, size, size), F32),
            pltpu.VMEM((2 * size, size), F32),
            pltpu.SemaphoreType.REGULAR((2,)),
            dma((2,)),
            dma((2,)),
            dma((2,)),
            dma((1,)),
            dma((CHUNKS,)),
            dma((ROUNDS, CHUNKS, groups - 1)),
            dma((ROUNDS, CHUNKS, groups)),
            dma((CHUNKS,)),
            dma((CHUNKS,)),
            dma((2,)),
            dma((2,)),
            dma((3,)),
            dma((3,)),
            dma((stages, 2)),
            dma((stages, 2)),
            dma((2, stages // 2, 3)),
            dma((2, stages // 2, 3)),
            dma((1,)),
            dma((1,)),
            dma((2,)),
            dma((2,)),
        ],
        compiler_params=pltpu.CompilerParams(
            collective_id=0, has_side_effects=True, vmem_limit_bytes=30 * 1024 * 1024
        ),
    )(*(pltpu.with_memory_space_constraint(x, pltpu.HBM) for x in (factor, support.T, plan)))


def solution(mesh):
    return jax.shard_map(
        functools.partial(on_device, mesh.shape["col"], mesh.shape["row"]),
        mesh=mesh,
        in_specs=(P("row", "col"), P(None, "row"), P()),
        out_specs=P("row", "col"),
        check_vma=False,
    )
```

```python
import functools

import jax
import jax.numpy as jnp
from jax import lax
from jax.experimental import pallas as pl
from jax.experimental.pallas import tpu as pltpu
from jax.sharding import PartitionSpec as P

W = 128
RB = 128
ROUNDS = 2
CHUNKS = 2
STEPS = 7
DAMPING = 0.01
RELAY = 160
TOP = 2020.0
F32 = jnp.float32
BF16 = jnp.bfloat16
MESH = pl.DeviceIdType.MESH


def split(x):
    high = x.astype(BF16)
    return high, (x - high.astype(F32)).astype(BF16)


def dot(a, b):
    return jnp.dot(a, b, preferred_element_type=F32)


def dot3(a, b):
    a_high, a_low = split(a)
    b_high, b_low = split(b)
    return dot(a_high, b_high) + (dot(a_high, b_low) + dot(a_low, b_high))


def dot_t(a, b):
    return lax.dot_general(a, b, (((0,), (0,)), ((), ())), preferred_element_type=F32)


def rotation(gram, eye, stack):
    size = gram.shape[0]
    on_diagonal = gram * eye
    diag_rows = jnp.sum(on_diagonal, axis=1, keepdims=True)
    diag_cols = jnp.sum(on_diagonal, axis=0, keepdims=True)
    spread = diag_rows - diag_cols
    joined = diag_rows + diag_cols
    half = 0.5 * gram * spread / (spread * spread + gram * gram + DAMPING * joined * joined)
    squared = dot3(half, half)
    stack[:size] = eye - squared
    stack[size:] = eye - half
    scales, low, high = [], 1.0, TOP
    for _ in range(STEPS):
        scales.append(2.0 / (low + high))
        low, high = 4.0 * low * high / (low + high) ** 2, 1.0

    def factor(scale):
        return (2.0 * scale) * eye - (scale * scale) * stack[:size]

    def scaled(step, carry):
        scale = jnp.float32(scales[0])
        for i in range(1, STEPS - 1):
            scale = jnp.where(step == i, scales[i], scale)
        stack[...] = dot3(stack[...], factor(scale))
        return carry

    lax.fori_loop(0, STEPS - 1, scaled, 0)
    inverse = dot3(stack[size:], factor(scales[-1]))
    residual = (eye - inverse) - dot3(half, inverse)
    short = residual.astype(BF16)
    inverse = inverse + dot3(inverse, residual + dot(short, short))
    return 2.0 * inverse - eye


def pack(gram):
    first, last = gram[:W, :W], gram[W:, W:]
    row_ids = lax.broadcasted_iota(jnp.int32, (W, W), 0)
    col_ids = lax.broadcasted_iota(jnp.int32, (W, W), 1)
    tile = jnp.where(row_ids >= col_ids, first, last)
    diagonal = jnp.sum(jnp.where(row_ids == col_ids, last, 0.0), axis=0, keepdims=True)
    return gram[:W, W:], tile, jnp.broadcast_to(diagonal, (8, W))


def unpack(cross, tile, diagonal):
    row_ids = lax.broadcasted_iota(jnp.int32, (W, W), 0)
    col_ids = lax.broadcasted_iota(jnp.int32, (W, W), 1)
    lower = jnp.where(row_ids > col_ids, tile, 0.0)
    upper = jnp.where(row_ids < col_ids, tile, 0.0)
    first = lower + lower.T + jnp.where(row_ids == col_ids, tile, 0.0)
    last = upper + upper.T + jnp.where(row_ids == col_ids, diagonal, 0.0)
    top = jnp.concatenate([first, cross], axis=1)
    return jnp.concatenate([top, jnp.concatenate([cross.T, last], axis=1)], axis=0)


def kernel(
    groups, members, factor_ref, support_ref, plan_ref, out_ref,
    held, cur, send, recv, late, relay, halves, raw_out, raw_in, turn_out, turn, acc, gram, gram_in,
    piece, piece_in, whole, rot, stack,
    go_sem, relay_send, relay_recv, pass_send, pass_recv, load_sem, move_send, move_recv, raw_send, raw_recv, turn_send, turn_recv, swap_send, swap_recv, sum_send, sum_recv, quad_send, quad_recv, rot_send, rot_recv, whole_send, whole_recv,
):
    slots, rows, _ = cur.shape
    size = 2 * W
    chunk = rows // CHUNKS
    chips = members // 2
    stages = chips.bit_length() - 1
    g = lax.axis_index("col")
    m = lax.axis_index("row")
    core = lax.rem(m, 2)
    chip = m // 2
    partner = m + 1 - 2 * core
    half = g // 2
    at_end = jnp.logical_or(g == 0, g == groups - 1)
    inside = jnp.logical_not(at_end)
    goals = [2 - half, g + 1 - 2 * lax.rem(g, 2), 3 - 3 * half]

    def flipped(bit):
        step = 1 << bit
        on = lax.rem(chip // step, 2)
        return (chip + step - 2 * step * on) * 2 + core

    loads = []
    for q in range(CHUNKS):
        span = pl.ds(q * chunk, chunk)
        loads.append(pltpu.make_async_copy(factor_ref.at[span], held.at[span], load_sem.at[q]))
        loads[q].start()

    goal_peers = [{"col": goal, "row": m} for goal in goals]
    row_peers = [{"col": g, "row": partner}]
    row_peers += [{"col": g, "row": flipped(b)} for b in range(stages)]
    quads = stages // 2
    quad_peers = []
    for b in range(quads):
        one, two = flipped(b), flipped(b + quads)
        quad_peers.append([{"col": g, "row": other} for other in (one, two, one + two - m)])
    diagonals = [quad[2] for quad in quad_peers]
    barrier = pltpu.get_barrier_semaphore()
    for peer in goal_peers + row_peers + diagonals:
        pl.semaphore_signal(barrier, inc=1, device_id=peer, device_id_type=MESH)

    row_ids = lax.broadcasted_iota(jnp.int32, (size, size), 0)
    col_ids = lax.broadcasted_iota(jnp.int32, (size, size), 1)
    eye = (row_ids == col_ids).astype(F32)

    def mask(q):
        loads[q].wait()
        for s in range(slots):
            for b in range(q * chunk // RB, (q + 1) * chunk // RB):
                span = pl.ds(b * RB, RB)
                weight = support_ref[b, g * slots + s].astype(F32)
                cur[s, span] = held[span, s * W:(s + 1) * W] * weight

    def before(r, position):
        return position if r == 0 else plan_ref[r - 1, position]

    blocks = groups * slots
    pick, keep, take = [], [], []
    for r in range(ROUNDS):
        dest = []
        for s in range(slots):
            block = before(r, g * slots + s)
            dest.append(sum(
                jnp.where(plan_ref[r, j] == block, j // slots, 0) for j in range(blocks)))

        def slot_for(goal):
            return jnp.minimum(slots - 1, sum(
                jnp.where(dest[s] == goal, s, 0) for s in range(slots)))

        pick.append([slot_for(goal) for goal in goals])
        keep.append(slot_for(g))
        take.append([])
        for s in range(slots):
            block = plan_ref[r, g * slots + s]
            take[r].append(jnp.minimum(groups - 1, sum(
                jnp.where(before(r, j) == block, j // slots, 0) for j in range(blocks))))

    copies = []

    def start(copy):
        copy.start()
        copies.append(copy)
        return copy

    def move(r, q, j, source, last=False):
        count = chunk - RELAY if last and q == CHUNKS - 1 else chunk
        landing = late[q] if last else recv[r][q].at[source]
        return pltpu.make_async_remote_copy(
            src_ref=send.at[r, j, pl.ds(q * chunk, count)],
            dst_ref=landing.at[pl.ds(0, count)],
            send_sem=move_send.at[r, q, j],
            recv_sem=move_recv.at[r, q, source],
            device_id=goal_peers[j],
            device_id_type=MESH,
        )

    across = (0, groups - 2)
    relays = [pltpu.make_async_remote_copy(
        src_ref=send.at[1, j, pl.ds(rows - RELAY, RELAY)],
        dst_ref=relay.at[i],
        send_sem=relay_send.at[i],
        recv_sem=relay_recv.at[i],
        device_id=goal_peers[1],
        device_id_type=MESH,
    ) for i, j in enumerate(across)]
    passes = [pltpu.make_async_remote_copy(
        src_ref=relay.at[i],
        dst_ref=late[CHUNKS - 1].at[pl.ds(chunk - RELAY, RELAY)],
        send_sem=pass_send.at[i],
        recv_sem=pass_recv.at[0],
        device_id=goal_peers[j],
        device_id_type=MESH,
    ) for i, j in enumerate(across)]

    def prepare(r, q):
        span = pl.ds(q * chunk, chunk)
        for j in range(groups - 1):
            send[r, j, span] = cur[pick[r][j], span]
        recv[r][q][g] = cur[keep[r], span]

    def arrive_first(q):
        for source in goals:
            move(0, q, 0, source).wait_recv()

    def arrive_early(q):
        move(1, q, 0, goals[0]).wait_recv()

        @pl.when(at_end)
        def _():
            move(1, q, 0, goals[1]).wait_recv()

    def arrive_late(q):
        move(1, q, 0, goals[2], True).wait_recv()
        if q == CHUNKS - 1:
            passes[0].wait_recv()

    raws = [pltpu.make_async_remote_copy(
        src_ref=raw_out.at[q],
        dst_ref=raw_in.at[q],
        send_sem=raw_send.at[q],
        recv_sem=raw_recv.at[q],
        device_id=goal_peers[1],
        device_id_type=MESH,
    ) for q in range(CHUNKS)]
    near_slot = pick[1][1]
    share = pl.ds(pl.multiple_of(core * W, W), W)
    turn_copy = pltpu.make_async_remote_copy(
        src_ref=turn_out,
        dst_ref=turn.at[share],
        send_sem=turn_send.at[0],
        recv_sem=turn_recv.at[0],
        device_id=goal_peers[1],
        device_id_type=MESH,
    )
    turn_swap = pltpu.make_async_remote_copy(
        src_ref=turn.at[share],
        dst_ref=turn.at[share],
        send_sem=turn_send.at[1],
        recv_sem=turn_recv.at[1],
        device_id=row_peers[0],
        device_id_type=MESH,
    )

    def start_raw(q):
        @pl.when(at_end)
        def _():
            raw_out[q] = load_pair(near_slot // 2, q)
            raws[q].start()

    def start_turn():
        @pl.when(at_end)
        def _():
            side = jnp.where(near_slot // 2 == core, 0, 1)
            wide = rot[side, share]
            turn_out[...] = jnp.where(lax.rem(near_slot, 2) == 0, wide[:, :W], wide[:, W:])
            turn_copy.start()

    def turn_raws():
        @pl.when(inside)
        def _():
            turn_copy.wait_recv()
            turn_swap.start()
            turn_swap.wait_recv()
            for q in range(CHUNKS):
                raws[q].wait_recv()
                recv[1][q][goals[1]] = dot3(raw_in[q], turn[...])

    def start_second(q):
        @pl.when(inside)
        def _():
            for j in (*across, 1):
                move(1, q, j, g).start()

        if q == CHUNKS - 1:
            @pl.when(at_end)
            def _():
                for copy in relays:
                    copy.start()

    def start_far():
        @pl.when(inside)
        def _():
            for q in range(CHUNKS):
                for j in across:
                    move(1, q, j, g).wait_send()
            pl.semaphore_signal(go_sem.at[1], inc=1, device_id=goal_peers[1], device_id_type=MESH)
            for i in range(2):
                relays[i].wait_recv()
                passes[i].start()

        @pl.when(at_end)
        def _():
            pl.semaphore_wait(go_sem.at[1], 1)
            for q in range(CHUNKS):
                for j in across:
                    move(1, q, j, g, True).start()

    def load_pair(k, q):
        first = jnp.where(k == 0, take[0][0], take[0][2])
        last = jnp.where(k == 0, take[0][1], take[0][3])
        return jnp.concatenate([recv[0][q][first], recv[0][q][last]], axis=1)

    far = goals[2]
    late_last = jnp.logical_or(take[1][2] == far, take[1][3] == far)
    late_pair = [jnp.where(late_last, take[1][2 + i], take[1][i]) for i in range(2)]
    early_pair = [jnp.where(late_last, take[1][i], take[1][2 + i]) for i in range(2)]
    far_left = late_pair[0] == far
    late_other = jnp.where(far_left, late_pair[1], late_pair[0])

    def load_early(q):
        return jnp.concatenate([recv[1][q][block] for block in early_pair], axis=1)

    def load_late(q):
        newest, other = late[q][...], recv[1][q][late_other]
        left, right = jnp.where(far_left, newest, other), jnp.where(far_left, other, newest)
        return jnp.concatenate([left, right], axis=1)

    def add_gram(k, q, pair):
        high, low = split(pair)
        mixed = dot_t(high, low)
        part = dot_t(high, high) + (mixed + mixed.T)
        acc[k] = part if q == 0 else acc[k] + part

    def sum_chips(total, slots_ref, cut):
        for stage in range(stages):
            slots_ref[2 * stage] = total
            both = []
            for h in range(2):
                bit = (stage + h * (stages // 2)) % stages
                part = pl.ds(0, cut) if h == 0 else pl.ds(cut, total.shape[0] - cut)
                both.append(start(pltpu.make_async_remote_copy(
                    src_ref=slots_ref.at[2 * stage, part],
                    dst_ref=slots_ref.at[2 * stage + 1, part],
                    send_sem=sum_send.at[stage, h],
                    recv_sem=sum_recv.at[stage, h],
                    device_id=row_peers[1 + bit],
                    device_id_type=MESH,
                )))
            for copy in both:
                copy.wait_recv()
            total = total + slots_ref[2 * stage + 1]
        return total

    def sum_quads(e, total):
        for step in range(quads):
            piece[e, 4 * step] = total
            three = [start(pltpu.make_async_remote_copy(
                src_ref=piece.at[e, 4 * step],
                dst_ref=piece.at[e, 4 * step + 1 + i],
                send_sem=quad_send.at[e, step, i],
                recv_sem=quad_recv.at[e, step, i],
                device_id=quad_peers[step][i],
                device_id_type=MESH,
            )) for i in (2, 0, 1)]
            for copy in three:
                copy.wait_recv()
            pair, other = (piece[e, 4 * step + 2 * i] + piece[e, 4 * step + 2 * i + 1] for i in range(2))
            total = pair + other
        return total

    def rotation_of(e):
        cross, tile, diagonal = pack(acc[e])
        piece_in[e, 0, :W] = cross
        piece_in[e, 0, W:] = diagonal
        piece_in[e, 1, :W] = tile
        piece_in[e, 1, W:] = diagonal
        start(pltpu.make_async_remote_copy(
            src_ref=piece_in.at[e, 1 - core],
            dst_ref=piece_in.at[e, 2],
            send_sem=swap_send.at[1 + e],
            recv_sem=swap_recv.at[1 + e],
            device_id=row_peers[0],
            device_id_type=MESH,
        )).wait_recv()
        total = sum_quads(e, piece_in[e, core] + piece_in[e, 2])
        whole[e, core] = total
        start(pltpu.make_async_remote_copy(
            src_ref=whole.at[e, core],
            dst_ref=whole.at[e, core],
            send_sem=whole_send.at[e],
            recv_sem=whole_recv.at[e],
            device_id=row_peers[0],
            device_id_type=MESH,
        )).wait_recv()
        return rotation(unpack(whole[e, 0, :W], whole[e, 1, :W], whole[e, 0, W:W + 1]), eye, stack)

    mask(0)
    prepare(0, 0)
    pl.semaphore_wait(barrier, groups - 1 + len(row_peers) + quads)
    for q in range(CHUNKS):
        if q:
            mask(q)
            prepare(0, q)
        for j in range(groups - 2):
            start(move(0, q, j, g))
    @pl.when(at_end)
    def _():
        pl.semaphore_wait(go_sem.at[0], 1)
        for q in range(CHUNKS):
            move(0, q, groups - 2, g).start()

    for q in range(CHUNKS):
        arrive_first(q)
        if q == CHUNKS - 2:
            @pl.when(inside)
            def _():
                for c in range(CHUNKS):
                    move(0, c, groups - 2, g).start()
        if q == CHUNKS - 1:
            @pl.when(inside)
            def _():
                pl.semaphore_signal(go_sem.at[0], inc=1, device_id=goal_peers[1], device_id_type=MESH)
        start_raw(q)
        for k in range(2):
            add_gram(k, q, load_pair(k, q))
    for k in range(2):
        cross, tile, diagonal = pack(acc[k])
        gram_in[k, :W] = cross
        gram_in[k, W:size] = tile
        gram_in[k, size:] = diagonal
    start(pltpu.make_async_remote_copy(
        src_ref=gram_in.at[1 - core],
        dst_ref=gram_in.at[2],
        send_sem=swap_send.at[0],
        recv_sem=swap_recv.at[0],
        device_id=row_peers[0],
        device_id_type=MESH,
    )).wait_recv()
    total = sum_chips(gram_in[core] + gram_in[2], gram, W)
    rot[0] = rotation(unpack(total[:W], total[W:size], total[size:size + 1]), eye, stack)
    back = start(pltpu.make_async_remote_copy(
        src_ref=rot.at[0],
        dst_ref=rot.at[1],
        send_sem=rot_send.at[0],
        recv_sem=rot_recv.at[0],
        device_id=row_peers[0],
        device_id_type=MESH,
    ))
    for side in range(2):
        k = core if side == 0 else 1 - core
        if side == 1:
            back.wait_recv()
        for q in (CHUNKS - 1, *range(CHUNKS - 1)):
            span = pl.ds(q * chunk, chunk)
            turned = dot3(load_pair(k, q), rot[side])
            cur[2 * k, span] = turned[:, :W]
            cur[2 * k + 1, span] = turned[:, W:]
            if side == 1:
                prepare(1, q)
                start_second(q)
                if q == CHUNKS - 1:
                    start_turn()

    start_far()
    turn_raws()
    for q in range(CHUNKS):
        arrive_early(q)
        add_gram(0, q, load_early(q))
    early = rotation_of(0)
    for q in range(CHUNKS):
        held[pl.ds(q * chunk, chunk), :size] = dot3(load_early(q), early)
    for q in range(CHUNKS):
        arrive_late(q)
        pair = load_late(q)
        add_gram(1, q, pair)
        halves[0, q], halves[1, q] = split(pair)
    last_high, last_low = split(rotation_of(1))
    for q in range(CHUNKS):
        span = pl.ds(q * chunk, chunk)
        high, low, ready = halves[0, q], halves[1, q], held[span, :size]
        turned = dot(high, last_high) + (dot(high, last_low) + dot(low, last_high))
        out_ref[span, :size] = jnp.where(late_last, ready, turned)
        out_ref[span, size:] = jnp.where(late_last, turned, ready)
    @pl.when(at_end)
    def _():
        for copy in [*raws, turn_copy]:
            copy.wait_send()

    @pl.when(inside)
    def _():
        turn_swap.wait_send()
        for copy in passes:
            copy.wait_send()
        for q in range(CHUNKS):
            move(1, q, 1, g).wait_send()

    for q in range(CHUNKS):
        move(0, q, groups - 2, g).wait_send()

    @pl.when(at_end)
    def _():
        for q in range(CHUNKS):
            for j in across:
                move(1, q, j, g, True).wait_send()
        for copy in relays:
            copy.wait_send()

    for copy in copies:
        copy.wait_send()


def on_device(groups, members, factor, support, plan):
    rows = factor.shape[0]
    slots = factor.shape[1] // W
    chips = members // 2
    stages = chips.bit_length() - 1
    assert slots == 4 and groups == 4 and chips == 1 << stages and stages % 2 == 0 and ROUNDS == 2
    size = 2 * W
    dma = pltpu.SemaphoreType.DMA
    smem = pl.BlockSpec(memory_space=pltpu.SMEM)
    return pl.pallas_call(
        functools.partial(kernel, groups, members),
        out_shape=jax.ShapeDtypeStruct(factor.shape, F32),
        in_specs=[pl.BlockSpec(memory_space=pl.ANY), smem, smem],
        out_specs=pl.BlockSpec(memory_space=pltpu.VMEM),
        scratch_shapes=[
            pltpu.VMEM(factor.shape, F32),
            pltpu.VMEM((slots, rows, W), F32),
            pltpu.VMEM((ROUNDS, groups - 1, rows, W), F32),
            [[pltpu.VMEM((groups, rows // CHUNKS, W), F32)] * CHUNKS] * ROUNDS,
            [pltpu.VMEM((rows // CHUNKS, W), F32)] * CHUNKS,
            pltpu.VMEM((2, RELAY, W), F32),
            pltpu.VMEM((2, CHUNKS, rows // CHUNKS, size), BF16),
            pltpu.VMEM((CHUNKS, rows // CHUNKS, size), F32),
            pltpu.VMEM((CHUNKS, rows // CHUNKS, size), F32),
            pltpu.VMEM((W, W), F32),
            pltpu.VMEM((size, W), F32),
            pltpu.VMEM((2, size, size), F32),
            pltpu.VMEM((2 * stages, size + 8, W), F32),
            pltpu.VMEM((3, size + 8, W), F32),
            pltpu.VMEM((2, 2 * stages, W + 8, W), F32),
            pltpu.VMEM((2, 3, W + 8, W), F32),
            pltpu.VMEM((2, 2, W + 8, W), F32),
            pltpu.VMEM((2, size, size), F32),
            pltpu.VMEM((2 * size, size), F32),
            pltpu.SemaphoreType.REGULAR((2,)),
            dma((2,)),
            dma((2,)),
            dma((2,)),
            dma((1,)),
            dma((CHUNKS,)),
            dma((ROUNDS, CHUNKS, groups - 1)),
            dma((ROUNDS, CHUNKS, groups)),
            dma((CHUNKS,)),
            dma((CHUNKS,)),
            dma((2,)),
            dma((2,)),
            dma((3,)),
            dma((3,)),
            dma((stages, 2)),
            dma((stages, 2)),
            dma((2, stages // 2, 3)),
            dma((2, stages // 2, 3)),
            dma((1,)),
            dma((1,)),
            dma((2,)),
            dma((2,)),
        ],
        compiler_params=pltpu.CompilerParams(
            collective_id=0, has_side_effects=True, vmem_limit_bytes=30 * 1024 * 1024
        ),
    )(*(pltpu.with_memory_space_constraint(x, pltpu.HBM) for x in (factor, support.T, plan)))


def solution(mesh):
    return jax.shard_map(
        functools.partial(on_device, mesh.shape["col"], mesh.shape["row"]),
        mesh=mesh,
        in_specs=(P("row", "col"), P(None, "row"), P()),
        out_specs=P("row", "col"),
        check_vma=False,
    )
```
